128 devices in a mesh: dp: 16 (over y, x), mp: 8 (over z, core).
Axes of the slice: x: 4, y: 4, z: 4, core: 2. Of those that a mesh axis runs over, the one named last changes fastest.
Arguments:
- queries: bfloat16 [32, 512, 8192], P('dp', None, 'mp'), may hold values from -6 to 6
- features: bfloat16 [32, 512, 8192], P('dp', None, 'mp'), may hold values from -6 to 6
- key_weight: bfloat16 [8192, 1024], P(('mp', 'dp')), may hold values from -0.0625 to 0.0625
- value_weight: bfloat16 [8192, 1024], P(('mp', 'dp')), may hold values from -0.0625 to 0.0625
- query_gain: float32 [128], replicated, may hold values from 0.1 to 1.9
- key_gain: float32 [128], replicated, may hold values from 0.1 to 1.9
- tile_count: int32 [32], P('dp'), may hold values from 1 to 4, as said below
- image_seq: int32 [32], P('dp'), may hold values from 0 to 1
- text_len: int32 [32], P('dp'), may hold values from 1 to 512, as said below
- cotangent: bfloat16 [32, 512, 8192], P('dp', None, 'mp'), may hold values from -6 to 6
Outputs:
- context: bfloat16 [32, 512, 8192], P('dp', None, 'mp')
- query_grad: bfloat16 [32, 512, 8192], P('dp', None, 'mp')
- feature_grad: bfloat16 [32, 512, 8192], P('dp', None, 'mp')
- key_weight_grad: float32 [8192, 1024], P(('mp', 'dp'))
- value_weight_grad: float32 [8192, 1024], P(('mp', 'dp'))
The draws below stay inside these ranges and needn't reach their ends.
Inputs may be any that keep to these rules, and one draw needn't show every extreme that they name: tile_count[i] tiles of image i hold data, the rest of its 512 slots are padding; some image has 4 tiles. Image i belongs to sequence 2 * (i // 2) + image_seq[i]; a sequence may have several images or none. Text tokens from text_len[s] on are padding; some sequence fills all 512 slots.
All inputs are finite; a program needn't handle non-finite values.
Results may differ from the reference program's by a relative error of at most 0.02.
Values may be sent and summed in bfloat16 or wider, within the bound.
A program may use at most 192 MiB of HBM per device.

```python
import math
import jax
import jax.numpy as jnp
from jax import lax

HEADS = 64
KV_HEADS = 8
HEAD_DIM = 128
D_IMG = 8192
TMAX = 4
TT = 128
IMG_DEV = 2
L = 512
IMAGES = 32
SEQS = 32
N_DP = 16


def draw_tile_count(key, part):
    key = jax.random.fold_in(key, 7)
    first_key, second_key = jax.random.split(key)
    counts = jax.random.randint(first_key, (IMAGES,), 1, TMAX + 1)
    chosen = jax.random.randint(second_key, (), 0, IMAGES)
    return jnp.where(jnp.arange(IMAGES) == chosen, TMAX, counts).astype(jnp.int32)


def draw_text_len(key, part):
    key = jax.random.fold_in(key, 13)
    first_key, second_key = jax.random.split(key)
    counts = jax.random.randint(first_key, (SEQS,), 1, L + 1)
    chosen = jax.random.randint(second_key, (), 0, SEQS)
    return jnp.where(jnp.arange(SEQS) == chosen, L, counts).astype(jnp.int32)


def place_ends(result, key, smallest, high):
    shape = result.shape
    place = [jax.random.randint(jax.random.fold_in(key, axis), (), 0, shape[axis]) for axis in range(len(shape))]
    result = result.at[tuple(place)].set(smallest)
    longest = shape.index(max(shape))
    place[longest] = (place[longest] + 1) % shape[longest]
    return result.at[tuple(place)].set(high)


def levels(rng, shape, cuts, least, high):
    gain, own = 1.0, jax.random.fold_in(rng, 6)
    for dim, shards_of in cuts:
        steps = jnp.exp(jax.random.uniform(jax.random.fold_in(own, dim), (shards_of,), jnp.float32, least / len(cuts), high / len(cuts)))
        gain = gain * jnp.repeat(steps, shape[dim] // shards_of).reshape([-1 if axis == dim else 1 for axis in range(len(shape))])
    return gain


def scatter_about(stream_key, extent, spread, reach, cuts=(), kind=jnp.bfloat16):
    values = jax.random.normal(stream_key, extent, jnp.float32) * spread
    if len(cuts) > 0:
        values = levels(stream_key, extent, cuts, -0.22, 0.18) * values
    return jnp.clip(values, min=-reach, max=reach).astype(kind)


def setup_inputs(seed: int = 0) -> dict:
    key_of = jax.random.split(jax.random.key(seed), 11)
    queries = scatter_about(key_of[0], (SEQS, L, HEADS * HEAD_DIM), 1.0, 6.0, ((0, 16), (2, 8)))
    features = scatter_about(key_of[1], (IMAGES, TMAX * TT, D_IMG), 1.0, 6.0, ((0, 16), (2, 8)))
    key_weight = scatter_about(key_of[2], (D_IMG, KV_HEADS * HEAD_DIM), D_IMG ** -0.5, 0.0625, ((0, 128),))
    value_weight = scatter_about(key_of[3], (D_IMG, KV_HEADS * HEAD_DIM), D_IMG ** -0.5, 0.0625, ((0, 128),))
    query_gain = jnp.clip(1.0 + 0.18 * jax.random.normal(key_of[4], (HEAD_DIM,), jnp.float32), 0.1, 1.9)
    key_gain = jnp.clip(1.0 + 0.18 * jax.random.normal(key_of[5], (HEAD_DIM,), jnp.float32), 0.1, 1.9)
    tile_count = draw_tile_count(jax.random.fold_in(key_of[10], 71), 0)
    image_seq = place_ends(jax.random.randint(key_of[7], (IMAGES,), 0, IMG_DEV), jax.random.fold_in(key_of[7], 1), 0, IMG_DEV - 1).astype(jnp.int32)
    text_len = draw_text_len(jax.random.fold_in(key_of[10], 71), 0)
    cotangent = scatter_about(key_of[9], (SEQS, L, HEADS * HEAD_DIM), 1.0, 6.0, ((0, 16), (2, 8)))
    return {"queries": queries, "features": features, "key_weight": key_weight, "value_weight": value_weight, "query_gain": query_gain, "key_gain": key_gain, "tile_count": tile_count, "image_seq": image_seq, "text_len": text_len, "cotangent": cotangent}


EPSILON = 1e-05

def normalize(values, gain_vec):
    root_mean = jnp.sqrt(lax.optimization_barrier(jnp.mean(values * values, axis=-1, keepdims=True)) + EPSILON)
    return (gain_vec * values / root_mean, root_mean)

def normalize_back(values, root_mean, gain_vec, grad_in):
    weighted = gain_vec * grad_in
    inner_sum = lax.optimization_barrier(jnp.sum(weighted * values, axis=-1, keepdims=True))
    return weighted / root_mean - values * inner_sum / (values.shape[-1] * root_mean * root_mean * root_mean)

def rounded(values):
    return lax.optimization_barrier(values.astype(jnp.bfloat16)).astype(jnp.float32)

def reference(queries, features, key_weight, value_weight, query_gain, key_gain, tile_count, image_seq, text_len, cotangent):
    group_size = HEADS // KV_HEADS
    slot_count = TMAX * TT
    token_count = IMG_DEV * slot_count
    text_rows = IMG_DEV * L
    proj_cols = KV_HEADS * HEAD_DIM
    inv_root = 1.0 / math.sqrt(HEAD_DIM)

    def per_group(accums, inputs):
        group_query, group_feat, group_tiles, group_seq, group_len, group_grad = inputs
        flat_rows = group_feat.reshape(token_count, D_IMG)
        key_raw = jnp.dot(flat_rows, key_weight, preferred_element_type=jnp.float32).reshape(token_count, KV_HEADS, HEAD_DIM)
        value_f = rounded(jnp.dot(flat_rows, value_weight, preferred_element_type=jnp.float32)).reshape(token_count, KV_HEADS, HEAD_DIM)
        key_norm, key_root = normalize(key_raw, key_gain)
        key_f = rounded(key_norm)
        query_f = group_query.astype(jnp.float32).reshape(text_rows, KV_HEADS, group_size, HEAD_DIM)
        query_norm, query_root = normalize(query_f, query_gain)
        query_hat = rounded(query_norm)
        slot_ok = jnp.arange(slot_count, dtype=jnp.int32)[None, :] < (group_tiles * TT)[:, None]
        owners = group_seq[None, :] == jnp.arange(IMG_DEV, dtype=jnp.int32)[:, None]
        has_img = jnp.any(owners, axis=1)
        allowed = (owners[:, :, None] & slot_ok[None]).reshape(IMG_DEV, token_count)
        allowed = jnp.repeat(allowed, L, axis=0).astype(jnp.float32)
        row_ok = ((jnp.arange(L, dtype=jnp.int32)[None, :] < group_len[:, None]) & has_img[:, None]).reshape(text_rows).astype(jnp.float32)
        missing = jnp.repeat(1.0 - has_img.astype(jnp.float32), L)
        masked = group_grad.astype(jnp.float32).reshape(text_rows, KV_HEADS, group_size, HEAD_DIM) * row_ok[:, None, None, None]

        def per_head(head_in):
            head_query, head_key, head_value, head_grad = head_in
            scores = jnp.einsum('rgd,nd->grn', head_query, head_key) * inv_root
            weights_exp = jnp.exp(scores) * allowed[None]
            denom_sum = lax.optimization_barrier(jnp.sum(weights_exp, axis=-1, keepdims=True)) + missing[None, :, None]
            prob_f = rounded(weights_exp / denom_sum)
            head_context = jnp.einsum('grn,nd->rgd', prob_f, head_value) * row_ok[:, None, None]
            prob_grad = jnp.einsum('rgd,nd->grn', head_grad, head_value)
            inner_sum = lax.optimization_barrier(jnp.sum(prob_f * prob_grad, axis=-1, keepdims=True))
            dscore = rounded(prob_f * (prob_grad - inner_sum))
            dquery = jnp.einsum('grn,nd->rgd', dscore, head_key) * inv_root
            dkey = jnp.einsum('grn,rgd->nd', dscore, head_query) * inv_root
            dvalue = jnp.einsum('grn,rgd->nd', prob_f, head_grad)
            return (head_context, dquery, dkey, dvalue)
        head_context, dquery, dkey, dvalue = lax.map(per_head, (query_hat.transpose(1, 0, 2, 3), key_f.transpose(1, 0, 2), value_f.transpose(1, 0, 2), masked.transpose(1, 0, 2, 3)))
        group_context = head_context.transpose(1, 0, 2, 3).reshape(IMG_DEV, L, HEADS * HEAD_DIM).astype(jnp.bfloat16)
        group_qgrad = normalize_back(query_f, query_root, query_gain, dquery.transpose(1, 0, 2, 3)).reshape(IMG_DEV, L, HEADS * HEAD_DIM).astype(jnp.bfloat16)
        key_grad = normalize_back(key_raw, key_root, key_gain, dkey.transpose(1, 0, 2)).reshape(token_count, proj_cols).astype(jnp.bfloat16)
        value_grad = dvalue.transpose(1, 0, 2).reshape(token_count, proj_cols).astype(jnp.bfloat16)
        feat_grad = jnp.dot(key_grad, key_weight.T, preferred_element_type=jnp.float32) + jnp.dot(value_grad, value_weight.T, preferred_element_type=jnp.float32)
        feat_grad = feat_grad.astype(jnp.bfloat16).reshape(IMG_DEV, slot_count, D_IMG)
        key_acc = accums[0] + jnp.dot(flat_rows.T, key_grad, preferred_element_type=jnp.float32)
        value_acc = accums[1] + jnp.dot(flat_rows.T, value_grad, preferred_element_type=jnp.float32)
        return ((key_acc, value_acc), (group_context, group_qgrad, feat_grad))
    zero_grad = jnp.zeros((D_IMG, proj_cols), jnp.float32)
    inputs = (queries.reshape(N_DP, IMG_DEV, L, HEADS * HEAD_DIM), features.reshape(N_DP, IMG_DEV, slot_count, D_IMG), tile_count.reshape(N_DP, IMG_DEV), image_seq.reshape(N_DP, IMG_DEV), text_len.reshape(N_DP, IMG_DEV), cotangent.reshape(N_DP, IMG_DEV, L, HEADS * HEAD_DIM))
    (key_weight_grad, value_weight_grad), (context, query_grad, feature_grad) = lax.scan(per_group, (zero_grad, zero_grad), inputs)
    context = context.reshape(SEQS, L, HEADS * HEAD_DIM)
    query_grad = query_grad.reshape(SEQS, L, HEADS * HEAD_DIM)
    feature_grad = feature_grad.reshape(IMAGES, slot_count, D_IMG)
    return (context, query_grad, feature_grad, key_weight_grad, value_weight_grad)
```

```python
import functools
import math

import jax
import jax.numpy as jnp
from jax import lax
from jax.experimental import pallas as pl
from jax.experimental.pallas import tpu as pltpu
from jax.sharding import PartitionSpec as P

KV_HEADS = 8
TT = 128
EPSILON = 1e-05
MESH = pl.DeviceIdType.MESH
BF = jnp.bfloat16
F32 = jnp.float32
MESSAGES = 320


def dot_nn(a, b):
    return jnp.dot(a, b, preferred_element_type=F32)


def dot_nt(a, b):
    return lax.dot_general(a, b, (((1,), (1,)), ((), ())), preferred_element_type=F32)


def dot_tn(a, b):
    return lax.dot_general(a, b, (((0,), (0,)), ((), ())), preferred_element_type=F32)


def kernel(
    queries,
    features,
    key_weight,
    value_weight,
    query_gain,
    key_gain,
    tile_count,
    image_seq,
    text_len,
    cotangent,
    context_out,
    query_out,
    feature_out,
    key_w_out,
    value_w_out,
    fv,
    ft,
    qv,
    cv,
    qh,
    cotp,
    ev,
    wb,
    part_tx,
    part_rx,
    total,
    z_tx,
    z_rx,
    kh,
    vh,
    tok,
    dvacc,
    dkacc,
    dkv,
    gr,
    rx1a,
    rx1b,
    rx2a,
    rx2b,
    ctx_st,
    qg_st,
    fg_st,
    wg_st,
    send_sem,
    recv_sem,
    load_sem,
):
    dp, mp = lax.axis_index("dp"), lax.axis_index("mp")
    y, x = lax.div(dp, 4), lax.rem(dp, 4)
    z, core = lax.div(mp, 2), lax.rem(mp, 2)
    x1, x2, x3 = (lax.rem(x + k, 4) for k in (1, 2, 3))
    y1, y2, y3 = (lax.rem(y + k, 4) for k in (1, 2, 3))
    z1, z2, z3 = (lax.rem(z + k, 4) for k in (1, 2, 3))
    to_xp = {"dp": y * 4 + x1, "mp": mp}
    to_xm = {"dp": y * 4 + x3, "mp": mp}
    to_yp = {"dp": y1 * 4 + x, "mp": mp}
    to_ym = {"dp": y3 * 4 + x, "mp": mp}
    to_zp = {"dp": dp, "mp": z1 * 2 + core}
    to_zm = {"dp": dp, "mp": z3 * 2 + core}
    to_pt = {"dp": dp, "mp": z * 2 + 1 - core}
    scale = 1.0 / math.sqrt(128)
    count = [0]
    sent = []

    class Msg:
        def __init__(self, src, dst, dev, local):
            k = count[0]
            count[0] += 1
            self.copy = pltpu.make_async_remote_copy(
                src_ref=src,
                dst_ref=dst,
                send_sem=send_sem.at[k],
                recv_sem=recv_sem.at[k],
                device_id=dev,
                device_id_type=MESH,
            )
            self.local, self.dev, self.k = local, dev, k
            self.copy.start()
            sent.append(self.copy)

        def arrive(self):
            pltpu.make_async_remote_copy(
                src_ref=self.local,
                dst_ref=self.local,
                send_sem=send_sem.at[self.k],
                recv_sem=recv_sem.at[self.k],
                device_id=self.dev,
                device_id_type=MESH,
            ).wait_recv()

    offs = (2, 1, 3, 0)
    own_loads = []
    for n in range(8):
        src = key_weight if n < 4 else value_weight
        zc = lax.rem(z + offs[n % 4], 4)
        for p in range(2):
            head = zc * 2 + (core if p == 0 else 1 - core)
            col = pl.multiple_of(head * 128, 128)
            c = pltpu.make_async_copy(
                src.at[:, pl.ds(col, 128)],
                wb.at[n, y, x, :, pl.ds(p * 128, 128)],
                load_sem.at[len(own_loads)],
            )
            c.start()
            own_loads.append(c)
    load_f = pltpu.make_async_copy(features, fv, load_sem.at[16])
    load_q = pltpu.make_async_copy(queries, qv, load_sem.at[17])
    load_c = pltpu.make_async_copy(cotangent, cv, load_sem.at[18])
    load_q.start()
    load_f.start()
    load_c.start()

    barrier = pltpu.get_barrier_semaphore()
    for dev in (to_xp, to_xm, to_yp, to_ym, to_zp, to_zm, to_pt):
        pl.semaphore_signal(barrier, inc=1, device_id=dev, device_id_type=MESH)
    pl.semaphore_wait(barrier, 7)

    first, second, group, far = {}, {}, {}, {}
    spans = {0: (0, 2), 1: (2, 2), 2: (4, 4)}

    def pa(span, xx):
        n0, cnt = span
        return wb.at[n0 : n0 + cnt, y, xx, 0:32]

    def pb(span, yy):
        n0, cnt = span
        return wb.at[n0 : n0 + cnt, yy, x, 32:64]

    def s0(k):
        sp = spans[k]
        first[k] = (
            Msg(pa(sp, x), pa(sp, x), to_xp, pa(sp, x3)),
            Msg(pa(sp, x), pa(sp, x), to_xm, pa(sp, x1)),
            Msg(pb(sp, y), pb(sp, y), to_yp, pb(sp, y3)),
            Msg(pb(sp, y), pb(sp, y), to_ym, pb(sp, y1)),
        )

    def s1(k):
        sp = spans[k]
        for msg in first[k]:
            msg.arrive()
        if k == 2:
            lo, hi = (4, 2), (6, 2)
            second[k] = (
                Msg(pa(lo, x3), pa(lo, x3), to_xp, pa(lo, x2)),
                Msg(pa(hi, x1), pa(hi, x1), to_xm, pa(hi, x2)),
                Msg(pb(lo, y3), pb(lo, y3), to_yp, pb(lo, y2)),
                Msg(pb(hi, y1), pb(hi, y1), to_ym, pb(hi, y2)),
            )
        elif k == 0:
            second[k] = (
                Msg(pa(sp, x3), pa(sp, x3), to_xp, pa(sp, x2)),
                Msg(pb(sp, y3), pb(sp, y3), to_yp, pb(sp, y2)),
            )
        else:
            second[k] = (
                Msg(pa(sp, x1), pa(sp, x1), to_xm, pa(sp, x2)),
                Msg(pb(sp, y1), pb(sp, y1), to_ym, pb(sp, y2)),
            )

    def s1b(k):
        for msg in second[k]:
            msg.arrive()

    def ga(n, yy, lo=0, hi=4):
        return wb.at[n, yy, lo:hi, 0:32]

    def gb(n, xx, lo=0, hi=4):
        return wb.at[n, lo:hi, xx, 32:64]

    def s2(n):
        group[n] = (
            Msg(ga(n, y), ga(n, y), to_yp, ga(n, y3)),
            Msg(ga(n, y), ga(n, y), to_ym, ga(n, y1)),
            Msg(gb(n, x), gb(n, x), to_xp, gb(n, x3)),
            Msg(gb(n, x), gb(n, x), to_xm, gb(n, x1)),
        )

    def s3(n):
        for msg in group[n]:
            msg.arrive()
        far[n] = (
            Msg(ga(n, y3, 0, 2), ga(n, y3, 0, 2), to_yp, ga(n, y2, 0, 2)),
            Msg(ga(n, y1, 2, 4), ga(n, y1, 2, 4), to_ym, ga(n, y2, 2, 4)),
            Msg(gb(n, x3, 0, 2), gb(n, x3, 0, 2), to_xp, gb(n, x2, 0, 2)),
            Msg(gb(n, x1, 2, 4), gb(n, x1, 2, 4), to_xm, gb(n, x2, 2, 4)),
        )

    def s4(n):
        for msg in far[n]:
            msg.arrive()

    part, r1, r2 = {}, {}, {}

    def t_of(n):
        return n % 4 if n % 4 < 3 else 3 + n // 4

    def proj(n):
        def block(i, carry):
            rows = pl.ds(pl.multiple_of(i * 256, 256), 256)
            out = dot_nn(fv[rows, :], wb[n].reshape(1024, 256))
            total[t_of(n), rows, :] = out[:, :128]
            part_tx[n, rows, :] = out[:, 128:].astype(BF)
            return carry

        lax.fori_loop(0, 4, block, 0)
        part[n] = Msg(part_tx.at[n], part_rx.at[n], to_pt, part_rx.at[n])

    def z_step(n):
        k, j, t = n // 4, n % 4, t_of(n)
        part[n].arrive()
        value = total[t] + part_rx[n].astype(F32)
        if j == 0:
            z_tx[k, 0] = value.astype(BF)
            up, down = (z_tx.at[k, 0, 0:512], z_rx.at[k, 0, 0:512]), (
                z_tx.at[k, 0, 512:1024],
                z_rx.at[k, 0, 512:1024],
            )
            r1[k] = (Msg(*up, to_zp, up[1]), Msg(*down, to_zm, down[1]))
        elif j == 1:
            r1[k][0].arrive()
            z_tx[k, 1, 0:512] = (value[:512] + z_rx[k, 0, 0:512].astype(F32)).astype(BF)
            z_tx[k, 1, 512:1024] = value[512:].astype(BF)
            r2[k] = [Msg(z_tx.at[k, 1], z_rx.at[k, 1], to_zp, z_rx.at[k, 1])]
        elif j == 2:
            r1[k][1].arrive()
            z_tx[k, 2, 0:512] = value[:512].astype(BF)
            z_tx[k, 2, 512:1024] = (value[512:] + z_rx[k, 0, 512:1024].astype(F32)).astype(BF)
            r2[k].append(Msg(z_tx.at[k, 2], z_rx.at[k, 2], to_zm, z_rx.at[k, 2]))
        else:
            total[t] = value
            for msg in r2[k]:
                msg.arrive()
            total[t] = total[t] + (z_rx[k, 1].astype(F32) + z_rx[k, 2].astype(F32))

    seqs = [image_seq[0], image_seq[1]]
    tiles = [tile_count[0], tile_count[1]]
    lens = [text_len[0], text_len[1]]
    own_len = [jnp.where(s == 0, lens[0], lens[1]) for s in seqs]
    same = jnp.where(seqs[0] == seqs[1], 1.0, 0.0).astype(F32)
    weight = [[jnp.where(seqs[i] == s, 1.0, 0.0).astype(F32) for s in range(2)] for i in range(2)]
    text_at = lax.broadcasted_iota(jnp.int32, (512, 128), 0)

    def norm_queries(s):
        gain = query_gain[...]

        def block(i, carry):
            rows = pl.ds(pl.multiple_of(i * 128, 128), 128)
            for g in range(8):
                q = qv[s, rows, g * 128 : (g + 1) * 128].astype(F32)
                inv = lax.rsqrt(jnp.mean(q * q, axis=-1, keepdims=True) + EPSILON)
                qh[s, g, rows, :] = (gain * q * inv).astype(BF)
            return carry

        lax.fori_loop(0, 4, block, 0)

    def turn_features():
        for i in range(4):
            ft[:, i * 256 : (i + 1) * 256] = fv[i * 256 : (i + 1) * 256, :].T

    def set_masks():
        for i in range(2):
            tok[i] = jnp.where(text_at < tiles[i] * TT, 1.0, 0.0).astype(BF)
            dvacc[i] = jnp.zeros((512, 128), F32)
            dkacc[i] = jnp.zeros((512, 128), F32)

    def key_final():
        raw = total[3]
        inv = lax.rsqrt(jnp.mean(raw * raw, axis=-1, keepdims=True) + EPSILON)
        kh[...] = (key_gain[...] * raw * inv).astype(BF).reshape(2, 512, 128)

    def value_final():
        vh[...] = total[4].astype(BF).reshape(2, 512, 128)

    def soft(g0, g1):
        def one(g, carry):
            den = []
            for i in range(2):
                q = qh[seqs[i], g]
                e = jnp.exp(dot_nt(q, kh[i]) * scale).astype(BF)
                ev[i, g] = e
                den.append(dot_nn(e, tok[i]))
            lane = pl.ds(pl.multiple_of(g * 128, 128), 128)
            for i in range(2):
                inv = 1.0 / (den[i] + same * den[1 - i])
                c = cv[seqs[i], :, lane].astype(F32) * inv
                c = jnp.where(text_at < own_len[i], c, 0.0).astype(BF)
                cotp[i, g] = c
                dvacc[i] += dot_tn(ev[i, g], c)
            return carry

        lax.fori_loop(g0, g1, one, 0)

    def back(g0, g1):
        def one(g, carry):
            lane = pl.ds(pl.multiple_of(g * 128, 128), 128)
            raw, den = [], []
            for i in range(2):
                both = dot_nn(ev[i, g], jnp.concatenate([vh[i] * tok[i], tok[i]], axis=1))
                raw.append(both[:, :128])
                den.append(both[:, 128:])
            ctx = [raw[i] / (den[i] + same * den[1 - i]) for i in range(2)]
            for s in range(2):
                out = weight[0][s] * ctx[0] + weight[1][s] * ctx[1]
                ctx_st[s, :, lane] = jnp.where(text_at < lens[s], out, 0.0).astype(BF)
            for i in range(2):
                c = cotp[i, g]
                inner = jnp.sum(
                    c.astype(F32) * (ctx[i] + same * ctx[1 - i]), axis=-1, keepdims=True
                )
                grad = dot_nt(c, vh[i])
                ds = (ev[i, g].astype(F32) * (grad - inner)).astype(BF)
                ev[i, g] = ds
                dkacc[i] += dot_tn(ds, qh[seqs[i], g])
            return carry

        lax.fori_loop(g0, g1, one, 0)

    def query_back(g0, g1):
        gain = query_gain[...]

        def one(g, carry):
            lane = pl.ds(pl.multiple_of(g * 128, 128), 128)
            dq = [dot_nn(ev[i, g], kh[i] * tok[i]) for i in range(2)]
            for s in range(2):
                got = gain * (weight[0][s] * dq[0] + weight[1][s] * dq[1]) * scale
                q = qv[s, :, lane].astype(F32)
                inv = lax.rsqrt(jnp.mean(q * q, axis=-1, keepdims=True) + EPSILON)
                inner = jnp.sum(got * q, axis=-1, keepdims=True)
                out = got * inv - q * (inner * (inv * inv * inv) * (1.0 / 128))
                qg_st[s, :, lane] = out.astype(BF)
            return carry

        lax.fori_loop(g0, g1, one, 0)

    near, across, over = {}, {}, {}

    def spread0(k):
        own = dkv.at[k, 0, 0]
        near[k] = (
            Msg(own, dkv.at[k, 1, 0], to_zp, dkv.at[k, 1, 0]),
            Msg(own, dkv.at[k, 2, 0], to_zm, dkv.at[k, 2, 0]),
        )
        across[k, 0] = Msg(own, dkv.at[k, 0, 1], to_pt, dkv.at[k, 0, 1])

    def spread1(k):
        near[k][0].arrive()
        slot = dkv.at[k, 3, 0, 0:512]
        up = Msg(dkv.at[k, 1, 0, 0:512], slot, to_zp, slot)
        across[k, 1] = Msg(dkv.at[k, 1, 0], dkv.at[k, 1, 1], to_pt, dkv.at[k, 1, 1])
        near[k][1].arrive()
        slot = dkv.at[k, 3, 0, 512:1024]
        down = Msg(dkv.at[k, 2, 0, 512:1024], slot, to_zm, slot)
        across[k, 2] = Msg(dkv.at[k, 2, 0], dkv.at[k, 2, 1], to_pt, dkv.at[k, 2, 1])
        over[k] = (up, down)

    def spread2(k):
        for msg in over[k]:
            msg.arrive()
        across[k, 3] = Msg(dkv.at[k, 3, 0], dkv.at[k, 3, 1], to_pt, dkv.at[k, 3, 1])

    m1a, m1b, m2a, m2b = {}, {}, {}, {}

    def w_of(k, j):
        return (3, 2, 1, 0)[j] + (4 if k == 0 else 0)

    def grad(k, j):
        t = k * 4 + j
        across[k, j].arrive()

        def block(i, carry):
            rows = pl.ds(pl.multiple_of(i * 256, 256), 256)
            cat = jnp.concatenate([dkv[k, j, 0], dkv[k, j, 1]], axis=1)
            out = dot_nn(ft[rows, :], cat).astype(BF)
            gr[t, 0, i] = out[:, :128].reshape(4, 64, 128)
            gr[t, 1, i] = out[:, 128:].reshape(4, 64, 128)
            return carry

        lax.fori_loop(0, 4, block, 0)
        a, b = gr.at[t, 0], gr.at[t, 1]
        r = [[rx1a.at[t, h, e] for e in range(2)] for h in range(2)]
        m1a[t] = (
            Msg(a.at[y2, 0:2], r[0][0], to_yp, r[0][0]),
            Msg(a.at[y2, 2:4], r[0][1], to_ym, r[0][1]),
            Msg(b.at[0:2, x2], r[1][0], to_xp, r[1][0]),
            Msg(b.at[2:4, x2], r[1][1], to_xm, r[1][1]),
        )

    def add(ref, *others):
        value = ref[...].astype(F32)
        for o in others:
            value = value + o[...].astype(F32)
        ref[...] = value.astype(BF)

    def p1b(t):
        a, b = gr.at[t, 0], gr.at[t, 1]
        for msg in m1a[t]:
            msg.arrive()
        add(a.at[y1, 0:2], rx1a.at[t, 0, 0])
        add(a.at[y3, 2:4], rx1a.at[t, 0, 1])
        add(b.at[0:2, x1], rx1a.at[t, 1, 0])
        add(b.at[2:4, x3], rx1a.at[t, 1, 1])
        r = [[rx1b.at[t, h, e] for e in range(2)] for h in range(2)]
        m1b[t] = (
            Msg(a.at[y1], r[0][0], to_yp, r[0][0]),
            Msg(a.at[y3], r[0][1], to_ym, r[0][1]),
            Msg(b.at[:, x1], r[1][0], to_xp, r[1][0]),
            Msg(b.at[:, x3], r[1][1], to_xm, r[1][1]),
        )

    def p2a(t):
        a, b = gr.at[t, 0], gr.at[t, 1]
        for msg in m1b[t]:
            msg.arrive()
        add(a.at[y], rx1b.at[t, 0, 0], rx1b.at[t, 0, 1])
        add(b.at[:, x], rx1b.at[t, 1, 0], rx1b.at[t, 1, 1])
        r = [[rx2a.at[t, h, e] for e in range(2)] for h in range(2)]
        m2a[t] = (
            Msg(a.at[y, x2, 0:32], r[0][0], to_xp, r[0][0]),
            Msg(a.at[y, x2, 32:64], r[0][1], to_xm, r[0][1]),
            Msg(b.at[y2, x, 0:32], r[1][0], to_yp, r[1][0]),
            Msg(b.at[y2, x, 32:64], r[1][1], to_ym, r[1][1]),
        )

    def p2b(t):
        a, b = gr.at[t, 0], gr.at[t, 1]
        for msg in m2a[t]:
            msg.arrive()
        add(a.at[y, x1, 0:32], rx2a.at[t, 0, 0])
        add(a.at[y, x3, 32:64], rx2a.at[t, 0, 1])
        add(b.at[y1, x, 0:32], rx2a.at[t, 1, 0])
        add(b.at[y3, x, 32:64], rx2a.at[t, 1, 1])
        r = [[rx2b.at[t, h, e] for e in range(2)] for h in range(2)]
        m2b[t] = (
            Msg(a.at[y, x1], r[0][0], to_xp, r[0][0]),
            Msg(a.at[y, x3], r[0][1], to_xm, r[0][1]),
            Msg(b.at[y1, x], r[1][0], to_yp, r[1][0]),
            Msg(b.at[y3, x], r[1][1], to_ym, r[1][1]),
        )

    def p3(t):
        k, j = t // 4, t % 4
        for msg in m2b[t]:
            msg.arrive()
        zc = (z, z3, z1, z2)[j]
        for h in range(2):
            head = zc * 2 + (core if h == 0 else 1 - core)
            lane = pl.ds(pl.multiple_of(head * 128, 128), 128)
            wg_st[k, :, lane] = (
                gr[t, h, y, x].astype(F32)
                + rx2b[t, h, 0].astype(F32)
                + rx2b[t, h, 1].astype(F32)
            )

    def feature_back():
        def block(i, carry):
            rows = pl.ds(pl.multiple_of(i * 256, 256), 256)
            acc = None
            for k in range(2):
                for j in range(4):
                    cat = jnp.concatenate([dkv[k, j, 0, rows], dkv[k, j, 1, rows]], axis=1)
                    term = dot_nt(cat, wb[w_of(k, j)].reshape(1024, 256))
                    acc = term if acc is None else acc + term
            fg_st[rows, :] = acc.astype(BF)
            return carry

        lax.fori_loop(0, 4, block, 0)

    def value_grad():
        for i in range(2):
            dkv[0, 0, 0, i * 512 : (i + 1) * 512] = (dvacc[i] * tok[i].astype(F32)).astype(BF)

    def key_grad():
        gain = key_gain[...]
        for i in range(2):
            got = gain * (dkacc[i] * tok[i].astype(F32)) * scale
            raw = total[3, i * 512 : (i + 1) * 512]
            inv = lax.rsqrt(jnp.mean(raw * raw, axis=-1, keepdims=True) + EPSILON)
            inner = jnp.sum(got * raw, axis=-1, keepdims=True)
            out = got * inv - raw * (inner * (inv * inv * inv) * (1.0 / 128))
            dkv[1, 0, 0, i * 512 : (i + 1) * 512] = out.astype(BF)

    stores = []

    def store(src, dst):
        c = pltpu.make_async_copy(src, dst, load_sem.at[19 + len(stores)])
        c.start()
        stores.append(c)

    for c in own_loads:
        c.wait()
    s0(0)
    s0(1)
    set_masks()
    load_q.wait()
    norm_queries(0)
    s1(0)
    s0(2)
    s1b(0)
    s2(0)
    s2(1)
    s1(1)
    load_f.wait()
    turn_features()
    s1b(1)
    s2(2)
    s3(0)
    norm_queries(1)
    load_c.wait()
    for n in range(8):
        if n < 7:
            s3(n + 1)
        if n == 0:
            s1(2)
            s1b(2)
        if n < 5:
            s2(n + 3)
        s4(n)
        proj(n)
        if n > 0:
            z_step(n - 1)
        if n == 4:
            key_final()
        if n == 5:
            soft(0, 2)
        if n == 6:
            soft(2, 4)
        if n == 7:
            soft(4, 6)
    z_step(7)
    soft(6, 8)
    value_grad()
    spread0(0)
    value_final()
    grad(0, 0)
    back(0, 2)
    p1b(0)
    spread1(0)
    back(2, 4)
    grad(0, 1)
    grad(0, 2)
    p2a(0)
    spread2(0)
    back(4, 6)
    p1b(1)
    p1b(2)
    p2b(0)
    grad(0, 3)
    back(6, 8)
    key_grad()
    spread0(1)
    grad(1, 0)
    store(ctx_st, context_out)
    p2a(1)
    p2a(2)
    p1b(3)
    p3(0)
    p2b(1)
    p2b(2)
    p1b(4)
    query_back(0, 4)
    spread1(1)
    p2a(3)
    grad(1, 1)
    grad(1, 2)
    p2a(4)
    p3(1)
    p3(2)
    p2b(3)
    query_back(4, 8)
    store(qg_st, query_out)
    p1b(5)
    p1b(6)
    spread2(1)
    p2b(4)
    p3(3)
    grad(1, 3)
    p2a(5)
    p2a(6)
    feature_back()
    store(fg_st, feature_out)
    p1b(7)
    p3(4)
    p2b(5)
    p2b(6)
    p2a(7)
    p3(5)
    p3(6)
    p2b(7)
    p3(7)
    store(wg_st.at[0], value_w_out)
    store(wg_st.at[1], key_w_out)
    for c in sent:
        c.wait_send()
    for c in stores:
        c.wait()


def per_device(
    queries,
    features,
    key_weight,
    value_weight,
    query_gain,
    key_gain,
    tile_count,
    image_seq,
    text_len,
    cotangent,
):
    hbm = pl.BlockSpec(memory_space=pl.ANY)
    vmem = pl.BlockSpec(memory_space=pltpu.VMEM)
    smem = pl.BlockSpec(memory_space=pltpu.SMEM)
    v = pltpu.VMEM
    context, query_grad, feature_grad, key_w, value_w = pl.pallas_call(
        kernel,
        out_shape=(
            jax.ShapeDtypeStruct((2, 512, 1024), BF),
            jax.ShapeDtypeStruct((2, 512, 1024), BF),
            jax.ShapeDtypeStruct((1024, 1024), BF),
            jax.ShapeDtypeStruct((64, 1024), F32),
            jax.ShapeDtypeStruct((64, 1024), F32),
        ),
        in_specs=[hbm, hbm, hbm, hbm, vmem, vmem, smem, smem, smem, hbm],
        out_specs=(hbm,) * 5,
        scratch_shapes=[
            v((1024, 1024), BF),
            v((1024, 1024), BF),
            v((2, 512, 1024), BF),
            v((2, 512, 1024), BF),
            v((2, 8, 512, 128), BF),
            v((2, 8, 512, 128), BF),
            v((2, 8, 512, 512), BF),
            v((8, 4, 4, 64, 256), BF),
            v((8, 1024, 128), BF),
            v((8, 1024, 128), BF),
            v((5, 1024, 128), F32),
            v((2, 3, 1024, 128), BF),
            v((2, 3, 1024, 128), BF),
            v((2, 512, 128), BF),
            v((2, 512, 128), BF),
            v((2, 512, 128), BF),
            v((2, 512, 128), F32),
            v((2, 512, 128), F32),
            v((2, 4, 2, 1024, 128), BF),
            v((8, 2, 4, 4, 64, 128), BF),
            v((8, 2, 2, 2, 64, 128), BF),
            v((8, 2, 2, 4, 64, 128), BF),
            v((8, 2, 2, 32, 128), BF),
            v((8, 2, 2, 64, 128), BF),
            v((2, 512, 1024), BF),
            v((2, 512, 1024), BF),
            v((1024, 1024), BF),
            v((2, 64, 1024), F32),
            pltpu.SemaphoreType.DMA((MESSAGES,)),
            pltpu.SemaphoreType.DMA((MESSAGES,)),
            pltpu.SemaphoreType.DMA((32,)),
        ],
        compiler_params=pltpu.CompilerParams(
            collective_id=0, has_side_effects=True, vmem_limit_bytes=62 * 1024 * 1024
        ),
    )(
        queries,
        features.reshape(1024, 1024),
        key_weight,
        value_weight,
        query_gain.reshape(1, 128),
        key_gain.reshape(1, 128),
        tile_count,
        image_seq,
        text_len,
        cotangent,
    )
    return context, query_grad, feature_grad.reshape(2, 512, 1024), key_w, value_w


def solution(mesh):
    in_specs = (
        P("dp", None, "mp"),
        P("dp", None, "mp"),
        P(("mp", "dp"), None),
        P(("mp", "dp"), None),
        P(),
        P(),
        P("dp"),
        P("dp"),
        P("dp"),
        P("dp", None, "mp"),
    )
    out_specs = (
        P("dp", None, "mp"),
        P("dp", None, "mp"),
        P("dp", None, "mp"),
        P(("mp", "dp"), None),
        P(("mp", "dp"), None),
    )
    return jax.shard_map(
        per_device, mesh=mesh, in_specs=in_specs, out_specs=out_specs, check_vma=False
    )
```

```python
import functools
import math

import jax
import jax.numpy as jnp
from jax import lax
from jax.experimental import pallas as pl
from jax.experimental.pallas import tpu as pltpu
from jax.sharding import PartitionSpec as P

KV_HEADS = 8
TT = 128
EPSILON = 1e-05
MESH = pl.DeviceIdType.MESH
BF = jnp.bfloat16
F32 = jnp.float32
MESSAGES = 320
DIRECT = (0,)


def dot_nn(a, b):
    return jnp.dot(a, b, preferred_element_type=F32)


def dot_nt(a, b):
    return lax.dot_general(a, b, (((1,), (1,)), ((), ())), preferred_element_type=F32)


def dot_tn(a, b):
    return lax.dot_general(a, b, (((0,), (0,)), ((), ())), preferred_element_type=F32)


def kernel(
    queries,
    features,
    key_weight,
    value_weight,
    query_gain,
    key_gain,
    tile_count,
    image_seq,
    text_len,
    cotangent,
    context_out,
    query_out,
    feature_out,
    key_w_out,
    value_w_out,
    fv,
    ft,
    qv,
    cv,
    qh,
    cotp,
    ev,
    wb,
    part_tx,
    part_rx,
    total,
    z_tx,
    z_rx,
    kh,
    vh,
    tok,
    dvacc,
    dkacc,
    kt,
    vt,
    dkv,
    gr,
    rx1,
    rx2,
    inner,
    ctx_st,
    qg_st,
    fg_st,
    wg_st,
    send_sem,
    recv_sem,
    load_sem,
):
    dp, mp = lax.axis_index("dp"), lax.axis_index("mp")
    y, x = lax.div(dp, 4), lax.rem(dp, 4)
    z, core = lax.div(mp, 2), lax.rem(mp, 2)
    x1, x2, x3 = (lax.rem(x + k, 4) for k in (1, 2, 3))
    y1, y2, y3 = (lax.rem(y + k, 4) for k in (1, 2, 3))
    z1, z2, z3 = (lax.rem(z + k, 4) for k in (1, 2, 3))
    to_xp = {"dp": y * 4 + x1, "mp": mp}
    to_xm = {"dp": y * 4 + x3, "mp": mp}
    to_yp = {"dp": y1 * 4 + x, "mp": mp}
    to_ym = {"dp": y3 * 4 + x, "mp": mp}
    to_zp = {"dp": dp, "mp": z1 * 2 + core}
    to_zm = {"dp": dp, "mp": z3 * 2 + core}
    to_x2 = {"dp": y * 4 + x2, "mp": mp}
    to_y2 = {"dp": y2 * 4 + x, "mp": mp}
    to_z2 = {"dp": dp, "mp": z2 * 2 + core}
    to_pt = {"dp": dp, "mp": z * 2 + 1 - core}
    scale = 1.0 / math.sqrt(128)
    count = [0]
    sent = []

    class Msg:
        def __init__(self, src, dst, dev, local):
            k = count[0]
            count[0] += 1
            self.copy = pltpu.make_async_remote_copy(
                src_ref=src,
                dst_ref=dst,
                send_sem=send_sem.at[k],
                recv_sem=recv_sem.at[k],
                device_id=dev,
                device_id_type=MESH,
            )
            self.local, self.dev, self.k = local, dev, k
            self.copy.start()
            sent.append(self.copy)

        def arrive(self):
            pltpu.make_async_remote_copy(
                src_ref=self.local,
                dst_ref=self.local,
                send_sem=send_sem.at[self.k],
                recv_sem=recv_sem.at[self.k],
                device_id=self.dev,
                device_id_type=MESH,
            ).wait_recv()

    offs = (2, 1, 3, 0)
    own_loads = []
    for n in range(8):
        src = key_weight if n < 4 else value_weight
        zc = lax.rem(z + offs[n % 4], 4)
        for p in range(2):
            head = zc * 2 + (core if p == 0 else 1 - core)
            col = pl.multiple_of(head * 128, 128)
            c = pltpu.make_async_copy(
                src.at[:, pl.ds(col, 128)],
                wb.at[n, y, x, :, pl.ds(p * 128, 128)],
                load_sem.at[len(own_loads)],
            )
            c.start()
            own_loads.append(c)
    load_f = pltpu.make_async_copy(features, fv, load_sem.at[16])
    load_q = pltpu.make_async_copy(queries, qv, load_sem.at[17])
    load_c = pltpu.make_async_copy(cotangent, cv, load_sem.at[18])
    load_q.start()
    load_f.start()
    load_c.start()

    barrier = pltpu.get_barrier_semaphore()
    for dev in (to_xp, to_xm, to_x2, to_yp, to_ym, to_y2, to_zp, to_zm, to_z2, to_pt):
        pl.semaphore_signal(barrier, inc=1, device_id=dev, device_id_type=MESH)
    pl.semaphore_wait(barrier, 10)

    first, group, far = {}, {}, {}
    spans = ((0, 1), (1, 3), (4, 4))

    def pa(span, xx):
        n0, cnt = span
        return wb.at[n0 : n0 + cnt, y, xx, 0:32]

    def pb(span, yy):
        n0, cnt = span
        return wb.at[n0 : n0 + cnt, yy, x, 32:64]

    def s0(k):
        sp = spans[k]
        for c in own_loads[2 * sp[0] : 2 * (sp[0] + sp[1])]:
            c.wait()
        first[k] = (
            Msg(pa(sp, x), pa(sp, x), to_xp, pa(sp, x3)),
            Msg(pa(sp, x), pa(sp, x), to_xm, pa(sp, x1)),
            Msg(pb(sp, y), pb(sp, y), to_yp, pb(sp, y3)),
            Msg(pb(sp, y), pb(sp, y), to_ym, pb(sp, y1)),
            Msg(pa(sp, x), pa(sp, x), to_x2, pa(sp, x2)),
            Msg(pb(sp, y), pb(sp, y), to_y2, pb(sp, y2)),
        )

    def s1(k):
        for msg in first[k]:
            msg.arrive()

    def ga(n, yy, lo=0, hi=4):
        return wb.at[n, yy, lo:hi, 0:32]

    def gb(n, xx, lo=0, hi=4):
        return wb.at[n, lo:hi, xx, 32:64]

    def s2(n):
        group[n] = (
            Msg(ga(n, y), ga(n, y), to_yp, ga(n, y3)),
            Msg(ga(n, y), ga(n, y), to_ym, ga(n, y1)),
            Msg(gb(n, x), gb(n, x), to_xp, gb(n, x3)),
            Msg(gb(n, x), gb(n, x), to_xm, gb(n, x1)),
        )
        if n in DIRECT:
            far[n] = (
                Msg(ga(n, y), ga(n, y), to_y2, ga(n, y2)),
                Msg(gb(n, x), gb(n, x), to_x2, gb(n, x2)),
            )

    def s3(n):
        for msg in group[n]:
            msg.arrive()
        if n not in DIRECT:
            far[n] = (
                Msg(ga(n, y3, 0, 2), ga(n, y3, 0, 2), to_yp, ga(n, y2, 0, 2)),
                Msg(ga(n, y1, 2, 4), ga(n, y1, 2, 4), to_ym, ga(n, y2, 2, 4)),
                Msg(gb(n, x3, 0, 2), gb(n, x3, 0, 2), to_xp, gb(n, x2, 0, 2)),
                Msg(gb(n, x1, 2, 4), gb(n, x1, 2, 4), to_xm, gb(n, x2, 2, 4)),
            )

    def s4(n):
        for msg in far[n]:
            msg.arrive()

    part, sums = {}, {}

    def t_of(n):
        return n % 4 if n % 4 < 3 else 3 + n // 4

    def proj(n):
        def block(i, carry):
            rows = pl.ds(pl.multiple_of(i * 256, 256), 256)
            out = dot_nn(fv[rows, :], wb[n].reshape(1024, 256))
            total[t_of(n), rows, :] = out[:, :128]
            part_tx[n, rows, :] = out[:, 128:].astype(BF)
            return carry

        lax.fori_loop(0, 4, block, 0, unroll=True)
        part[n] = Msg(part_tx.at[n], part_rx.at[n], to_pt, part_rx.at[n])

    def z_step(n):
        k, j, t = n // 4, n % 4, t_of(n)
        part[n].arrive()
        value = total[t] + part_rx[n].astype(F32)
        if j < 3:
            z_tx[k, j] = value.astype(BF)
            sums[n] = Msg(z_tx.at[k, j], z_rx.at[k, j], (to_z2, to_zp, to_zm)[j], z_rx.at[k, j])
        else:
            total[t] = value

    def z_last(k):
        t = 3 + k
        for j in range(3):
            sums[4 * k + j].arrive()
        total[t] = total[t] + (
            z_rx[k, 0].astype(F32) + z_rx[k, 1].astype(F32) + z_rx[k, 2].astype(F32)
        )

    seqs = [image_seq[0], image_seq[1]]
    tiles = [tile_count[0], tile_count[1]]
    lens = [text_len[0], text_len[1]]
    own_len = [jnp.where(s == 0, lens[0], lens[1]) for s in seqs]
    same = jnp.where(seqs[0] == seqs[1], 1.0, 0.0).astype(F32)
    weight = [[jnp.where(seqs[i] == s, 1.0, 0.0).astype(F32) for s in range(2)] for i in range(2)]
    text_at = lax.broadcasted_iota(jnp.int32, (512, 128), 0)

    def norm_queries(s):
        gain = query_gain[...]

        def block(i, carry):
            rows = pl.ds(pl.multiple_of(i * 128, 128), 128)
            for g in range(8):
                q = qv[s, rows, g * 128 : (g + 1) * 128].astype(F32)
                inv = lax.rsqrt(jnp.mean(q * q, axis=-1, keepdims=True) + EPSILON)
                qh[s, g, rows, :] = (gain * q * inv).astype(BF)
            return carry

        lax.fori_loop(0, 4, block, 0, unroll=True)

    def turn_features():
        for i in range(4):
            ft[:, i * 256 : (i + 1) * 256] = fv[i * 256 : (i + 1) * 256, :].T

    def set_masks():
        for i in range(2):
            tok[i] = jnp.where(text_at < tiles[i] * TT, 1.0, 0.0).astype(BF)
            dvacc[i] = jnp.zeros((128, 512), F32)
            dkacc[i] = jnp.zeros((128, 512), F32)

    def key_final():
        raw = total[3]
        inv = lax.rsqrt(jnp.mean(raw * raw, axis=-1, keepdims=True) + EPSILON)
        kh[...] = (key_gain[...] * raw * inv).astype(BF).reshape(2, 512, 128)
        for i in range(2):
            kt[i] = kh[i].T

    def value_final():
        vh[...] = total[4].astype(BF).reshape(2, 512, 128)
        for i in range(2):
            vt[i] = vh[i].T

    def soft(g0, g1):
        def one(g, carry):
            den = []
            for i in range(2):
                q = qh[seqs[i], g]
                e = jnp.exp2(dot_nn(q, kt[i]) * (scale * 1.4426950408889634)).astype(BF)
                ev[i, g] = e
                den.append(dot_nn(e, tok[i]))
            lane = pl.ds(pl.multiple_of(g * 128, 128), 128)
            for i in range(2):
                inv = 1.0 / (den[i] + same * den[1 - i])
                c = cv[seqs[i], :, lane].astype(F32) * inv
                c = jnp.where(text_at < own_len[i], c, 0.0).astype(BF)
                cotp[i, g] = c
                dvacc[i] += dot_tn(c, ev[i, g])
            return carry

        lax.fori_loop(g0, g1, one, 0)

    def back_context(g0, g1):
        def one(g, carry):
            lane = pl.ds(pl.multiple_of(g * 128, 128), 128)
            raw, den = [], []
            for i in range(2):
                both = dot_nn(ev[i, g], jnp.concatenate([vh[i] * tok[i], tok[i]], axis=1))
                raw.append(both[:, :128])
                den.append(both[:, 128:])
            ctx = [raw[i] / (den[i] + same * den[1 - i]) for i in range(2)]
            for s in range(2):
                out = weight[0][s] * ctx[0] + weight[1][s] * ctx[1]
                ctx_st[s, :, lane] = jnp.where(text_at < lens[s], out, 0.0).astype(BF)
            for i in range(2):
                got = jnp.sum(
                    cotp[i, g].astype(F32) * (ctx[i] + same * ctx[1 - i]), axis=-1, keepdims=True
                )
                inner[i, g] = jnp.broadcast_to(got, (512, 128))
            return carry

        lax.fori_loop(g0, g1, one, 0)

    def back(i, g0, g1):
        def one(g, carry):
            grad_p = dot_nn(cotp[i, g], vt[i])
            less = jnp.concatenate([inner[i, g]] * 4, axis=1)
            ds = (ev[i, g].astype(F32) * (grad_p - less)).astype(BF)
            ev[i, g] = ds
            dkacc[i] += dot_tn(qh[seqs[i], g], ds)
            return carry

        lax.fori_loop(g0, g1, one, 0, unroll=2)

    def query_back(g0, g1):
        gain = query_gain[...]

        def one(g, carry):
            lane = pl.ds(pl.multiple_of(g * 128, 128), 128)
            dq = [dot_nn(ev[i, g], kh[i] * tok[i]) for i in range(2)]
            for s in range(2):
                got = gain * (weight[0][s] * dq[0] + weight[1][s] * dq[1]) * scale
                q = qv[s, :, lane].astype(F32)
                inv = lax.rsqrt(jnp.mean(q * q, axis=-1, keepdims=True) + EPSILON)
                dots = jnp.sum(got * q, axis=-1, keepdims=True)
                out = got * inv - q * (dots * (inv * inv * inv) * (1.0 / 128))
                qg_st[s, :, lane] = out.astype(BF)
            return carry

        lax.fori_loop(g0, g1, one, 0)

    near, across, over = {}, {}, {}

    def spread(k, i):
        r = slice(i * 512, (i + 1) * 512)
        own = dkv.at[k, 0, 0, r]
        near[k, i] = (
            Msg(own, dkv.at[k, 1, 0, r], to_zp, dkv.at[k, 1, 0, r]),
            Msg(own, dkv.at[k, 2, 0, r], to_zm, dkv.at[k, 2, 0, r]),
        )

    def spread_own(k):
        own = dkv.at[k, 0, 0]
        across[k, 0] = Msg(own, dkv.at[k, 0, 1], to_pt, dkv.at[k, 0, 1])
        over[k] = []

    def relay(k, i):
        for j, dev in ((1, to_zp), (2, to_zm)):
            near[k, i][j - 1].arrive()
            r = slice(i * 512 + (j - 1) * 256, i * 512 + j * 256)
            over[k].append(Msg(dkv.at[k, j, 0, r], dkv.at[k, 3, 0, r], dev, dkv.at[k, 3, 0, r]))

    def pass_near(k):
        for j in (1, 2):
            across[k, j] = Msg(dkv.at[k, j, 0], dkv.at[k, j, 1], to_pt, dkv.at[k, j, 1])

    def pass_far(k):
        for msg in over[k]:
            msg.arrive()
        across[k, 3] = Msg(dkv.at[k, 3, 0], dkv.at[k, 3, 1], to_pt, dkv.at[k, 3, 1])

    m1, m2 = {}, {}

    def w_of(k, j):
        return (3, 2, 1, 0)[j] + (4 if k == 0 else 0)

    def grad(k, j):
        t = k * 4 + j
        across[k, j].arrive()

        def block(i, carry):
            rows = pl.ds(pl.multiple_of(i * 256, 256), 256)
            cat = jnp.concatenate([dkv[k, j, 0], dkv[k, j, 1]], axis=1)
            out = dot_nn(ft[rows, :], cat).astype(BF)
            gr[t, 0, i] = out[:, :128].reshape(4, 64, 128)
            gr[t, 1, i] = out[:, 128:].reshape(4, 64, 128)
            return carry

        lax.fori_loop(0, 4, block, 0, unroll=True)
        a, b = gr.at[t, 0], gr.at[t, 1]
        r = [[rx1.at[t, h, e] for e in range(3)] for h in range(2)]
        m1[t] = (
            Msg(a.at[y1], r[0][0], to_yp, r[0][0]),
            Msg(a.at[y3], r[0][1], to_ym, r[0][1]),
            Msg(b.at[:, x1], r[1][0], to_xp, r[1][0]),
            Msg(b.at[:, x3], r[1][1], to_xm, r[1][1]),
            Msg(a.at[y2], r[0][2], to_y2, r[0][2]),
            Msg(b.at[:, x2], r[1][2], to_x2, r[1][2]),
        )

    def add(ref, h, t):
        value = ref[...].astype(F32)
        for e in range(3):
            value = value + rx1[t, h, e].astype(F32)
        ref[...] = value.astype(BF)

    def p2(t):
        a, b = gr.at[t, 0], gr.at[t, 1]
        for msg in m1[t]:
            msg.arrive()
        add(a.at[y], 0, t)
        add(b.at[:, x], 1, t)
        r = [[rx2.at[t, h, e] for e in range(3)] for h in range(2)]
        m2[t] = (
            Msg(a.at[y, x1], r[0][0], to_xp, r[0][0]),
            Msg(a.at[y, x3], r[0][1], to_xm, r[0][1]),
            Msg(b.at[y1, x], r[1][0], to_yp, r[1][0]),
            Msg(b.at[y3, x], r[1][1], to_ym, r[1][1]),
            Msg(a.at[y, x2], r[0][2], to_x2, r[0][2]),
            Msg(b.at[y2, x], r[1][2], to_y2, r[1][2]),
        )

    def p3(t):
        k, j = t // 4, t % 4
        for msg in m2[t]:
            msg.arrive()
        zc = (z, z3, z1, z2)[j]
        for h in range(2):
            head = zc * 2 + (core if h == 0 else 1 - core)
            lane = pl.ds(pl.multiple_of(head * 128, 128), 128)
            value = gr[t, h, y, x].astype(F32)
            for e in range(3):
                value = value + rx2[t, h, e].astype(F32)
            wg_st[k, :, lane] = value

    def feature_back():
        def block(i, carry):
            rows = pl.ds(pl.multiple_of(i * 256, 256), 256)
            acc = None
            for k in range(2):
                for j in range(4):
                    cat = jnp.concatenate([dkv[k, j, 0, rows], dkv[k, j, 1, rows]], axis=1)
                    term = dot_nt(cat, wb[w_of(k, j)].reshape(1024, 256))
                    acc = term if acc is None else acc + term
            fg_st[rows, :] = acc.astype(BF)
            return carry

        lax.fori_loop(0, 4, block, 0, unroll=True)

    def value_grad(i):
        dkv[0, 0, 0, i * 512 : (i + 1) * 512] = (dvacc[i].T * tok[i].astype(F32)).astype(BF)

    def key_grad(i):
        gain = key_gain[...]
        got = gain * (dkacc[i].T * tok[i].astype(F32)) * scale
        raw = total[3, i * 512 : (i + 1) * 512]
        inv = lax.rsqrt(jnp.mean(raw * raw, axis=-1, keepdims=True) + EPSILON)
        dots = jnp.sum(got * raw, axis=-1, keepdims=True)
        out = got * inv - raw * (dots * (inv * inv * inv) * (1.0 / 128))
        dkv[1, 0, 0, i * 512 : (i + 1) * 512] = out.astype(BF)

    stores = []

    def store(src, dst):
        c = pltpu.make_async_copy(src, dst, load_sem.at[19 + len(stores)])
        c.start()
        stores.append(c)

    s0(0)
    s0(1)
    set_masks()
    load_q.wait()
    norm_queries(0)
    s1(0)
    s2(0)
    s1(1)
    s2(1)
    s2(2)
    s2(3)
    s0(2)
    norm_queries(1)
    load_f.wait()
    turn_features()
    load_c.wait()
    s3(0)
    s4(0)
    proj(0)
    s3(1)
    z_step(0)
    s3(2)
    s4(1)
    proj(1)
    s3(3)
    s1(2)
    s2(4)
    s2(5)
    s4(2)
    proj(2)
    z_step(1)
    s4(3)
    proj(3)
    z_step(2)
    s2(6)
    s2(7)
    z_step(3)
    s3(4)
    s3(5)
    s4(4)
    proj(4)
    z_last(0)
    key_final()
    soft(0, 2)
    s3(6)
    s3(7)
    s4(5)
    proj(5)
    z_step(4)
    soft(2, 4)
    s4(6)
    proj(6)
    z_step(5)
    s4(7)
    proj(7)
    z_step(6)
    soft(4, 6)
    z_step(7)
    soft(6, 8)
    value_grad(0)
    spread(0, 0)
    value_grad(1)
    spread(0, 1)
    spread_own(0)
    z_last(1)
    value_final()
    grad(0, 0)
    back_context(0, 8)
    store(ctx_st, context_out)
    relay(0, 0)
    back(0, 0, 4)
    relay(0, 1)
    pass_near(0)
    back(0, 4, 8)
    key_grad(0)
    spread(1, 0)
    grad(0, 1)
    grad(0, 2)
    pass_far(0)
    p2(0)
    back(1, 0, 8)
    key_grad(1)
    spread(1, 1)
    spread_own(1)
    grad(1, 0)
    grad(0, 3)
    relay(1, 0)
    p2(1)
    query_back(0, 4)
    relay(1, 1)
    pass_near(1)
    p2(2)
    query_back(4, 8)
    store(qg_st, query_out)
    grad(1, 1)
    grad(1, 2)
    pass_far(1)
    p3(0)
    p3(1)
    p3(2)
    p2(4)
    p2(3)
    grad(1, 3)
    p3(4)
    p3(3)
    store(wg_st.at[0], value_w_out)
    feature_back()
    store(fg_st, feature_out)
    p2(5)
    p2(6)
    p3(5)
    p3(6)
    p2(7)
    p3(7)
    store(wg_st.at[1], key_w_out)
    for c in sent:
        c.wait_send()
    for c in stores:
        c.wait()


def finish_kernel(*refs):
    stage, sem = refs[10:15], refs[15]
    loads = [pltpu.make_async_copy(refs[k], stage[k], sem.at[0, k]) for k in range(5)]
    stores = [pltpu.make_async_copy(stage[k], refs[5 + k], sem.at[1, k]) for k in range(5)]
    for c in loads:
        c.start()
    for k in range(5):
        loads[k].wait()
        stores[k].start()
    for c in stores:
        c.wait()


def finish(*arrays):
    hbm = pl.BlockSpec(memory_space=pl.ANY)
    return pl.pallas_call(
        finish_kernel,
        out_shape=tuple(jax.ShapeDtypeStruct(a.shape, a.dtype) for a in arrays),
        in_specs=[hbm] * 5,
        out_specs=(hbm,) * 5,
        scratch_shapes=[pltpu.VMEM(a.shape, a.dtype) for a in arrays]
        + [pltpu.SemaphoreType.DMA((2, 5))],
        compiler_params=pltpu.CompilerParams(vmem_limit_bytes=60 * 1024 * 1024),
    )(*arrays)


def per_device(
    queries,
    features,
    key_weight,
    value_weight,
    query_gain,
    key_gain,
    tile_count,
    image_seq,
    text_len,
    cotangent,
):
    hbm = pl.BlockSpec(memory_space=pl.ANY)
    vmem = pl.BlockSpec(memory_space=pltpu.VMEM)
    smem = pl.BlockSpec(memory_space=pltpu.SMEM)
    v = pltpu.VMEM
    context, query_grad, feature_grad, key_w, value_w = pl.pallas_call(
        kernel,
        out_shape=(
            jax.ShapeDtypeStruct((2, 512, 1024), BF),
            jax.ShapeDtypeStruct((2, 512, 1024), BF),
            jax.ShapeDtypeStruct((1024, 1024), BF),
            jax.ShapeDtypeStruct((64, 1024), F32),
            jax.ShapeDtypeStruct((64, 1024), F32),
        ),
        in_specs=[hbm, hbm, hbm, hbm, vmem, vmem, smem, smem, smem, hbm],
        out_specs=(hbm,) * 5,
        scratch_shapes=[
            v((1024, 1024), BF),
            v((1024, 1024), BF),
            v((2, 512, 1024), BF),
            v((2, 512, 1024), BF),
            v((2, 8, 512, 128), BF),
            v((2, 8, 512, 128), BF),
            v((2, 8, 512, 512), BF),
            v((8, 4, 4, 64, 256), BF),
            v((8, 1024, 128), BF),
            v((8, 1024, 128), BF),
            v((5, 1024, 128), F32),
            v((2, 3, 1024, 128), BF),
            v((2, 3, 1024, 128), BF),
            v((2, 512, 128), BF),
            v((2, 512, 128), BF),
            v((2, 512, 128), BF),
            v((2, 128, 512), F32),
            v((2, 128, 512), F32),
            v((2, 128, 512), BF),
            v((2, 128, 512), BF),
            v((2, 4, 2, 1024, 128), BF),
            v((8, 2, 4, 4, 64, 128), BF),
            v((8, 2, 3, 4, 64, 128), BF),
            v((8, 2, 3, 64, 128), BF),
            v((2, 8, 512, 128), F32),
            v((2, 512, 1024), BF),
            v((2, 512, 1024), BF),
            v((1024, 1024), BF),
            v((2, 64, 1024), F32),
            pltpu.SemaphoreType.DMA((MESSAGES,)),
            pltpu.SemaphoreType.DMA((MESSAGES,)),
            pltpu.SemaphoreType.DMA((32,)),
        ],
        compiler_params=pltpu.CompilerParams(
            collective_id=0, has_side_effects=True, vmem_limit_bytes=62 * 1024 * 1024
        ),
    )(
        queries,
        features.reshape(1024, 1024),
        key_weight,
        value_weight,
        query_gain.reshape(1, 128),
        key_gain.reshape(1, 128),
        tile_count,
        image_seq,
        text_len,
        cotangent,
    )
    context, query_grad, feature_grad, key_w, value_w = finish(
        context, query_grad, feature_grad, key_w, value_w
    )
    return context, query_grad, feature_grad.reshape(2, 512, 1024), key_w, value_w


def solution(mesh):
    in_specs = (
        P("dp", None, "mp"),
        P("dp", None, "mp"),
        P(("mp", "dp"), None),
        P(("mp", "dp"), None),
        P(),
        P(),
        P("dp"),
        P("dp"),
        P("dp"),
        P("dp", None, "mp"),
    )
    out_specs = (
        P("dp", None, "mp"),
        P("dp", None, "mp"),
        P("dp", None, "mp"),
        P(("mp", "dp"), None),
        P(("mp", "dp"), None),
    )
    return jax.shard_map(
        per_device, mesh=mesh, in_specs=in_specs, out_specs=out_specs, check_vma=False
    )
```

```python
import functools
import math

import jax
import jax.numpy as jnp
from jax import lax
from jax.experimental import pallas as pl
from jax.experimental.pallas import tpu as pltpu
from jax.sharding import PartitionSpec as P

KV_HEADS = 8
TT = 128
EPSILON = 1e-05
MESH = pl.DeviceIdType.MESH
BF = jnp.bfloat16
F32 = jnp.float32
MESSAGES = 320
DIRECT = (0,)


def dot_nn(a, b):
    return jnp.dot(a, b, preferred_element_type=F32)


def dot_nt(a, b):
    return lax.dot_general(a, b, (((1,), (1,)), ((), ())), preferred_element_type=F32)


def dot_tn(a, b):
    return lax.dot_general(a, b, (((0,), (0,)), ((), ())), preferred_element_type=F32)


def kernel(
    queries,
    features,
    key_weight,
    value_weight,
    query_gain,
    key_gain,
    tile_count,
    image_seq,
    text_len,
    cotangent,
    context_out,
    query_out,
    feature_out,
    key_w_out,
    value_w_out,
    fv,
    ft,
    qv,
    cv,
    qh,
    cotp,
    ev,
    wb,
    part_tx,
    part_rx,
    total,
    z_tx,
    z_rx,
    kh,
    vh,
    tok,
    dvacc,
    dkacc,
    kt,
    vt,
    dkv,
    gr,
    rx1,
    rx2,
    inner,
    ctx_st,
    qg_st,
    fg_st,
    wg_st,
    send_sem,
    recv_sem,
    load_sem,
):
    dp, mp = lax.axis_index("dp"), lax.axis_index("mp")
    y, x = lax.div(dp, 4), lax.rem(dp, 4)
    z, core = lax.div(mp, 2), lax.rem(mp, 2)
    x1, x2, x3 = (lax.rem(x + k, 4) for k in (1, 2, 3))
    y1, y2, y3 = (lax.rem(y + k, 4) for k in (1, 2, 3))
    z1, z2, z3 = (lax.rem(z + k, 4) for k in (1, 2, 3))
    to_xp = {"dp": y * 4 + x1, "mp": mp}
    to_xm = {"dp": y * 4 + x3, "mp": mp}
    to_yp = {"dp": y1 * 4 + x, "mp": mp}
    to_ym = {"dp": y3 * 4 + x, "mp": mp}
    to_zp = {"dp": dp, "mp": z1 * 2 + core}
    to_zm = {"dp": dp, "mp": z3 * 2 + core}
    to_x2 = {"dp": y * 4 + x2, "mp": mp}
    to_y2 = {"dp": y2 * 4 + x, "mp": mp}
    to_z2 = {"dp": dp, "mp": z2 * 2 + core}
    to_pt = {"dp": dp, "mp": z * 2 + 1 - core}
    scale = 1.0 / math.sqrt(128)
    count = [0]
    sent = []

    class Msg:
        def __init__(self, src, dst, dev, local):
            k = count[0]
            count[0] += 1
            self.copy = pltpu.make_async_remote_copy(
                src_ref=src,
                dst_ref=dst,
                send_sem=send_sem.at[k],
                recv_sem=recv_sem.at[k],
                device_id=dev,
                device_id_type=MESH,
            )
            self.local, self.dev, self.k = local, dev, k
            self.copy.start()
            sent.append(self.copy)

        def arrive(self):
            pltpu.make_async_remote_copy(
                src_ref=self.local,
                dst_ref=self.local,
                send_sem=send_sem.at[self.k],
                recv_sem=recv_sem.at[self.k],
                device_id=self.dev,
                device_id_type=MESH,
            ).wait_recv()

    offs = (2, 1, 3, 0)
    own_loads = []
    for n in range(8):
        src = key_weight if n < 4 else value_weight
        zc = lax.rem(z + offs[n % 4], 4)
        for p in range(2):
            head = zc * 2 + (core if p == 0 else 1 - core)
            col = pl.multiple_of(head * 128, 128)
            c = pltpu.make_async_copy(
                src.at[:, pl.ds(col, 128)],
                wb.at[n, y, x, :, pl.ds(p * 128, 128)],
                load_sem.at[len(own_loads)],
            )
            c.start()
            own_loads.append(c)
    load_f = pltpu.make_async_copy(features, fv, load_sem.at[16])
    load_q = pltpu.make_async_copy(queries, qv, load_sem.at[17])
    load_c = pltpu.make_async_copy(cotangent, cv, load_sem.at[18])
    load_q.start()
    load_f.start()
    load_c.start()

    barrier = pltpu.get_barrier_semaphore()
    for dev in (to_xp, to_xm, to_x2, to_yp, to_ym, to_y2, to_zp, to_zm, to_z2, to_pt):
        pl.semaphore_signal(barrier, inc=1, device_id=dev, device_id_type=MESH)
    pl.semaphore_wait(barrier, 10)

    first, group, far = {}, {}, {}
    spans = ((0, 1), (1, 3), (4, 4))

    def pa(span, xx):
        n0, cnt = span
        return wb.at[n0 : n0 + cnt, y, xx, 0:32]

    def pb(span, yy):
        n0, cnt = span
        return wb.at[n0 : n0 + cnt, yy, x, 32:64]

    def s0(k):
        sp = spans[k]
        for c in own_loads[2 * sp[0] : 2 * (sp[0] + sp[1])]:
            c.wait()
        first[k] = (
            Msg(pa(sp, x), pa(sp, x), to_xp, pa(sp, x3)),
            Msg(pa(sp, x), pa(sp, x), to_xm, pa(sp, x1)),
            Msg(pb(sp, y), pb(sp, y), to_yp, pb(sp, y3)),
            Msg(pb(sp, y), pb(sp, y), to_ym, pb(sp, y1)),
            Msg(pa(sp, x), pa(sp, x), to_x2, pa(sp, x2)),
            Msg(pb(sp, y), pb(sp, y), to_y2, pb(sp, y2)),
        )

    def s1(k):
        for msg in first[k]:
            msg.arrive()

    def ga(n, yy, lo=0, hi=4):
        return wb.at[n, yy, lo:hi, 0:32]

    def gb(n, xx, lo=0, hi=4):
        return wb.at[n, lo:hi, xx, 32:64]

    def s2(n):
        group[n] = (
            Msg(ga(n, y), ga(n, y), to_yp, ga(n, y3)),
            Msg(ga(n, y), ga(n, y), to_ym, ga(n, y1)),
            Msg(gb(n, x), gb(n, x), to_xp, gb(n, x3)),
            Msg(gb(n, x), gb(n, x), to_xm, gb(n, x1)),
        )
        if n in DIRECT:
            far[n] = (
                Msg(ga(n, y), ga(n, y), to_y2, ga(n, y2)),
                Msg(gb(n, x), gb(n, x), to_x2, gb(n, x2)),
            )

    def s3(n):
        for msg in group[n]:
            msg.arrive()
        if n not in DIRECT:
            far[n] = (
                Msg(ga(n, y3, 0, 2), ga(n, y3, 0, 2), to_yp, ga(n, y2, 0, 2)),
                Msg(ga(n, y1, 2, 4), ga(n, y1, 2, 4), to_ym, ga(n, y2, 2, 4)),
                Msg(gb(n, x3, 0, 2), gb(n, x3, 0, 2), to_xp, gb(n, x2, 0, 2)),
                Msg(gb(n, x1, 2, 4), gb(n, x1, 2, 4), to_xm, gb(n, x2, 2, 4)),
            )

    def s4(n):
        for msg in far[n]:
            msg.arrive()

    part, sums = {}, {}

    def t_of(n):
        return n % 4 if n % 4 < 3 else 3 + n // 4

    def proj(n):
        def block(i, carry):
            rows = pl.ds(pl.multiple_of(i * 256, 256), 256)
            out = dot_nn(fv[rows, :], wb[n].reshape(1024, 256))
            total[t_of(n), rows, :] = out[:, :128]
            part_tx[n, rows, :] = out[:, 128:].astype(BF)
            return carry

        lax.fori_loop(0, 4, block, 0, unroll=True)
        part[n] = Msg(part_tx.at[n], part_rx.at[n], to_pt, part_rx.at[n])

    def z_step(n):
        k, j, t = n // 4, n % 4, t_of(n)
        part[n].arrive()
        value = total[t] + part_rx[n].astype(F32)
        total[t] = value
        if j == 0:
            z_tx[k, 0] = value.astype(BF)
            for h, dev in ((0, to_zp), (1, to_zm)):
                r = slice(h * 512, (h + 1) * 512)
                sums[k, 0, h] = Msg(z_tx.at[k, 0, r], z_rx.at[k, 0, r], dev, z_rx.at[k, 0, r])
        elif j < 3:
            h = 2 - j
            r = slice(h * 512, (h + 1) * 512)
            z_tx[k, j, r] = value[r].astype(BF)
            dev = (to_zp, to_zm)[j - 1]
            sums[k, j, h] = Msg(z_tx.at[k, j, r], z_rx.at[k, j, r], dev, z_rx.at[k, j, r])

    def z_relay(k):
        for h, dev in ((0, to_zp), (1, to_zm)):
            j = h + 1
            sums[k, 0, h].arrive()
            r = slice(h * 512, (h + 1) * 512)
            z_tx[k, j, r] = (total[j, r] + z_rx[k, 0, r].astype(F32)).astype(BF)
            sums[k, j, h] = Msg(z_tx.at[k, j, r], z_rx.at[k, j, r], dev, z_rx.at[k, j, r])

    def z_last(k):
        t = 3 + k
        for j in (1, 2):
            for h in range(2):
                sums[k, j, h].arrive()
        total[t] = total[t] + (z_rx[k, 1].astype(F32) + z_rx[k, 2].astype(F32))

    seqs = [image_seq[0], image_seq[1]]
    tiles = [tile_count[0], tile_count[1]]
    lens = [text_len[0], text_len[1]]
    own_len = [jnp.where(s == 0, lens[0], lens[1]) for s in seqs]
    same = jnp.where(seqs[0] == seqs[1], 1.0, 0.0).astype(F32)
    weight = [[jnp.where(seqs[i] == s, 1.0, 0.0).astype(F32) for s in range(2)] for i in range(2)]
    text_at = lax.broadcasted_iota(jnp.int32, (512, 128), 0)

    def norm_queries(s):
        gain = query_gain[...]

        def block(i, carry):
            rows = pl.ds(pl.multiple_of(i * 128, 128), 128)
            for g in range(8):
                q = qv[s, rows, g * 128 : (g + 1) * 128].astype(F32)
                inv = lax.rsqrt(jnp.mean(q * q, axis=-1, keepdims=True) + EPSILON)
                qh[s, g, rows, :] = (gain * q * inv).astype(BF)
            return carry

        lax.fori_loop(0, 4, block, 0, unroll=True)

    def turn_features():
        for i in range(4):
            ft[:, i * 256 : (i + 1) * 256] = fv[i * 256 : (i + 1) * 256, :].T

    def set_masks():
        for i in range(2):
            tok[i] = jnp.where(text_at < tiles[i] * TT, 1.0, 0.0).astype(BF)
            dvacc[i] = jnp.zeros((128, 512), F32)
            dkacc[i] = jnp.zeros((128, 512), F32)

    def key_final():
        raw = total[3]
        inv = lax.rsqrt(jnp.mean(raw * raw, axis=-1, keepdims=True) + EPSILON)
        kh[...] = (key_gain[...] * raw * inv).astype(BF).reshape(2, 512, 128)
        for i in range(2):
            kt[i] = kh[i].T

    def value_final():
        vh[...] = total[4].astype(BF).reshape(2, 512, 128)
        for i in range(2):
            vt[i] = vh[i].T

    def soft(g0, g1):
        def one(g, carry):
            den = []
            for i in range(2):
                q = qh[seqs[i], g]
                e = jnp.exp2(dot_nn(q, kt[i]) * (scale * 1.4426950408889634)).astype(BF)
                ev[i, g] = e
                den.append(dot_nn(e, tok[i]))
            lane = pl.ds(pl.multiple_of(g * 128, 128), 128)
            for i in range(2):
                inv = 1.0 / (den[i] + same * den[1 - i])
                inner[i, g] = inv
                c = cv[seqs[i], :, lane].astype(F32) * inv
                c = jnp.where(text_at < own_len[i], c, 0.0).astype(BF)
                cotp[i, g] = c
                dvacc[i] += dot_tn(c, ev[i, g])
            return carry

        lax.fori_loop(g0, g1, one, 0)

    def back_context(g0, g1):
        def one(g, carry):
            lane = pl.ds(pl.multiple_of(g * 128, 128), 128)
            ctx = [dot_nn(ev[i, g], vh[i] * tok[i]) * inner[i, g] for i in range(2)]
            for i in range(2):
                full = ctx[i] + same * ctx[1 - i]
                fg_st[i * 512 : (i + 1) * 512, lane] = full.astype(BF)
                got = jnp.sum(cotp[i, g].astype(F32) * full, axis=-1, keepdims=True)
                inner[i, g] = jnp.broadcast_to(got, (512, 128))
            return carry

        lax.fori_loop(g0, g1, one, 0)

    def context_final():
        def one(g, carry):
            lane = pl.ds(pl.multiple_of(g * 128, 128), 128)
            full = [fg_st[i * 512 : (i + 1) * 512, lane].astype(F32) for i in range(2)]
            for s in range(2):
                out = jnp.where(seqs[1] == s, full[1], 0.0)
                out = jnp.where(seqs[0] == s, full[0], out)
                ctx_st[s, :, lane] = jnp.where(text_at < lens[s], out, 0.0).astype(BF)
            return carry

        lax.fori_loop(0, 8, one, 0)

    def back(i, g0, g1):
        def one(g, carry):
            grad_p = dot_nn(cotp[i, g], vt[i])
            less = jnp.concatenate([inner[i, g]] * 4, axis=1)
            ds = (ev[i, g].astype(F32) * (grad_p - less)).astype(BF)
            ev[i, g] = ds
            dkacc[i] += dot_tn(qh[seqs[i], g], ds)
            return carry

        lax.fori_loop(g0, g1, one, 0, unroll=2)

    def query_back(g0, g1):
        gain = query_gain[...]

        def one(g, carry):
            lane = pl.ds(pl.multiple_of(g * 128, 128), 128)
            dq = [dot_nn(ev[i, g], kh[i] * tok[i]) for i in range(2)]
            for s in range(2):
                got = gain * (weight[0][s] * dq[0] + weight[1][s] * dq[1]) * scale
                q = qv[s, :, lane].astype(F32)
                inv = lax.rsqrt(jnp.mean(q * q, axis=-1, keepdims=True) + EPSILON)
                dots = jnp.sum(got * q, axis=-1, keepdims=True)
                out = got * inv - q * (dots * (inv * inv * inv) * (1.0 / 128))
                qg_st[s, :, lane] = out.astype(BF)
            return carry

        lax.fori_loop(g0, g1, one, 0)

    near, across, over = {}, {}, {}

    def spread(k, i):
        r = slice(i * 512, (i + 1) * 512)
        own = dkv.at[k, 0, 0, r]
        near[k, i] = (
            Msg(own, dkv.at[k, 1, 0, r], to_zp, dkv.at[k, 1, 0, r]),
            Msg(own, dkv.at[k, 2, 0, r], to_zm, dkv.at[k, 2, 0, r]),
        )

    def spread_own(k):
        own = dkv.at[k, 0, 0]
        across[k, 0] = Msg(own, dkv.at[k, 0, 1], to_pt, dkv.at[k, 0, 1])
        over[k] = []

    def relay(k, i):
        for j, dev in ((1, to_zp), (2, to_zm)):
            near[k, i][j - 1].arrive()
            r = slice(i * 512 + (j - 1) * 256, i * 512 + j * 256)
            over[k].append(Msg(dkv.at[k, j, 0, r], dkv.at[k, 3, 0, r], dev, dkv.at[k, 3, 0, r]))

    def pass_near(k):
        for j in (1, 2):
            across[k, j] = Msg(dkv.at[k, j, 0], dkv.at[k, j, 1], to_pt, dkv.at[k, j, 1])

    def pass_far(k):
        for msg in over[k]:
            msg.arrive()
        across[k, 3] = Msg(dkv.at[k, 3, 0], dkv.at[k, 3, 1], to_pt, dkv.at[k, 3, 1])

    m1, m2 = {}, {}

    def w_of(k, j):
        return (3, 2, 1, 0)[j] + (4 if k == 0 else 0)

    def grad(k, j):
        t = k * 4 + j
        across[k, j].arrive()

        def block(i, carry):
            rows = pl.ds(pl.multiple_of(i * 256, 256), 256)
            cat = jnp.concatenate([dkv[k, j, 0], dkv[k, j, 1]], axis=1)
            out = dot_nn(ft[rows, :], cat).astype(BF)
            gr[t, 0, i] = out[:, :128].reshape(4, 64, 128)
            gr[t, 1, i] = out[:, 128:].reshape(4, 64, 128)
            return carry

        lax.fori_loop(0, 4, block, 0, unroll=True)
        a, b = gr.at[t, 0], gr.at[t, 1]
        r = [[rx1.at[t, h, e] for e in range(3)] for h in range(2)]
        m1[t] = (
            Msg(a.at[y1], r[0][0], to_yp, r[0][0]),
            Msg(a.at[y3], r[0][1], to_ym, r[0][1]),
            Msg(b.at[:, x1], r[1][0], to_xp, r[1][0]),
            Msg(b.at[:, x3], r[1][1], to_xm, r[1][1]),
            Msg(a.at[y2], r[0][2], to_y2, r[0][2]),
            Msg(b.at[:, x2], r[1][2], to_x2, r[1][2]),
        )

    def add(ref, h, t):
        value = ref[...].astype(F32)
        for e in range(3):
            value = value + rx1[t, h, e].astype(F32)
        ref[...] = value.astype(BF)

    def p2(t):
        a, b = gr.at[t, 0], gr.at[t, 1]
        for msg in m1[t]:
            msg.arrive()
        add(a.at[y], 0, t)
        add(b.at[:, x], 1, t)
        r = [[rx2.at[t, h, e] for e in range(3)] for h in range(2)]
        m2[t] = (
            Msg(a.at[y, x1], r[0][0], to_xp, r[0][0]),
            Msg(a.at[y, x3], r[0][1], to_xm, r[0][1]),
            Msg(b.at[y1, x], r[1][0], to_yp, r[1][0]),
            Msg(b.at[y3, x], r[1][1], to_ym, r[1][1]),
            Msg(a.at[y, x2], r[0][2], to_x2, r[0][2]),
            Msg(b.at[y2, x], r[1][2], to_y2, r[1][2]),
        )

    def p3(t):
        k, j = t // 4, t % 4
        for msg in m2[t]:
            msg.arrive()
        zc = (z, z3, z1, z2)[j]
        for h in range(2):
            head = zc * 2 + (core if h == 0 else 1 - core)
            lane = pl.ds(pl.multiple_of(head * 128, 128), 128)
            value = gr[t, h, y, x].astype(F32)
            for e in range(3):
                value = value + rx2[t, h, e].astype(F32)
            wg_st[k, :, lane] = value

    def feature_back(i0, i1):
        def block(i, carry):
            rows = pl.ds(pl.multiple_of(i * 256, 256), 256)
            acc = None
            for k in range(2):
                for j in range(4):
                    cat = jnp.concatenate([dkv[k, j, 0, rows], dkv[k, j, 1, rows]], axis=1)
                    term = dot_nt(cat, wb[w_of(k, j)].reshape(1024, 256))
                    acc = term if acc is None else acc + term
            fg_st[rows, :] = acc.astype(BF)
            return carry

        lax.fori_loop(i0, i1, block, 0, unroll=True)

    def value_grad(i):
        dkv[0, 0, 0, i * 512 : (i + 1) * 512] = (dvacc[i].T * tok[i].astype(F32)).astype(BF)

    def key_grad(i):
        gain = key_gain[...]
        got = gain * (dkacc[i].T * tok[i].astype(F32)) * scale
        raw = total[3, i * 512 : (i + 1) * 512]
        inv = lax.rsqrt(jnp.mean(raw * raw, axis=-1, keepdims=True) + EPSILON)
        dots = jnp.sum(got * raw, axis=-1, keepdims=True)
        out = got * inv - raw * (dots * (inv * inv * inv) * (1.0 / 128))
        dkv[1, 0, 0, i * 512 : (i + 1) * 512] = out.astype(BF)

    stores = []

    def store(src, dst):
        c = pltpu.make_async_copy(src, dst, load_sem.at[19 + len(stores)])
        c.start()
        stores.append(c)

    s0(0)
    s0(1)
    set_masks()
    load_q.wait()
    norm_queries(0)
    s1(0)
    s2(0)
    s1(1)
    s2(1)
    s2(2)
    s2(3)
    s0(2)
    norm_queries(1)
    load_f.wait()
    turn_features()
    load_c.wait()
    s3(0)
    s4(0)
    proj(0)
    s3(1)
    z_step(0)
    s3(2)
    s4(1)
    proj(1)
    s3(3)
    s1(2)
    s2(4)
    s2(5)
    s4(2)
    proj(2)
    z_step(1)
    s4(3)
    proj(3)
    z_step(2)
    z_relay(0)
    s2(6)
    s2(7)
    z_step(3)
    s3(4)
    s3(5)
    s4(4)
    proj(4)
    z_last(0)
    key_final()
    soft(0, 2)
    s3(6)
    s3(7)
    s4(5)
    proj(5)
    z_step(4)
    soft(2, 4)
    s4(6)
    proj(6)
    z_step(5)
    s4(7)
    proj(7)
    z_step(6)
    z_relay(1)
    soft(4, 6)
    z_step(7)
    soft(6, 8)
    value_grad(0)
    spread(0, 0)
    value_grad(1)
    spread(0, 1)
    spread_own(0)
    z_last(1)
    value_final()
    grad(0, 0)
    back_context(0, 8)
    relay(0, 0)
    back(0, 0, 4)
    relay(0, 1)
    pass_near(0)
    back(0, 4, 8)
    key_grad(0)
    spread(1, 0)
    grad(0, 1)
    grad(0, 2)
    pass_far(0)
    p2(0)
    back(1, 0, 8)
    key_grad(1)
    spread(1, 1)
    spread_own(1)
    grad(1, 0)
    relay(1, 0)
    grad(0, 3)
    p2(1)
    query_back(0, 4)
    relay(1, 1)
    pass_near(1)
    p2(2)
    context_final()
    store(ctx_st, context_out)
    grad(1, 1)
    grad(1, 2)
    pass_far(1)
    p2(3)
    p2(4)
    grad(1, 3)
    p3(0)
    p3(1)
    p3(2)
    p2(5)
    query_back(4, 8)
    store(qg_st, query_out)
    p3(3)
    p3(4)
    store(wg_st.at[0], value_w_out)
    feature_back(0, 2)
    store(fg_st.at[0:512], feature_out.at[0:512])
    p2(6)
    p2(7)
    feature_back(2, 4)
    store(fg_st.at[512:1024], feature_out.at[512:1024])
    p3(5)
    p3(6)
    p3(7)
    store(wg_st.at[1], key_w_out)
    for c in sent:
        c.wait_send()
    for c in stores:
        c.wait()


def finish_kernel(*refs):
    stage, sem = refs[10:15], refs[15]
    loads = [pltpu.make_async_copy(refs[k], stage[k], sem.at[0, k]) for k in range(5)]
    stores = [pltpu.make_async_copy(stage[k], refs[5 + k], sem.at[1, k]) for k in range(5)]
    for c in loads:
        c.start()
    for k in range(5):
        loads[k].wait()
        stores[k].start()
    for c in stores:
        c.wait()


def finish(*arrays):
    hbm = pl.BlockSpec(memory_space=pl.ANY)
    return pl.pallas_call(
        finish_kernel,
        out_shape=tuple(jax.ShapeDtypeStruct(a.shape, a.dtype) for a in arrays),
        in_specs=[hbm] * 5,
        out_specs=(hbm,) * 5,
        scratch_shapes=[pltpu.VMEM(a.shape, a.dtype) for a in arrays]
        + [pltpu.SemaphoreType.DMA((2, 5))],
        compiler_params=pltpu.CompilerParams(vmem_limit_bytes=60 * 1024 * 1024),
    )(*arrays)


def per_device(
    queries,
    features,
    key_weight,
    value_weight,
    query_gain,
    key_gain,
    tile_count,
    image_seq,
    text_len,
    cotangent,
):
    hbm = pl.BlockSpec(memory_space=pl.ANY)
    vmem = pl.BlockSpec(memory_space=pltpu.VMEM)
    smem = pl.BlockSpec(memory_space=pltpu.SMEM)
    v = pltpu.VMEM
    context, query_grad, feature_grad, key_w, value_w = pl.pallas_call(
        kernel,
        out_shape=(
            jax.ShapeDtypeStruct((2, 512, 1024), BF),
            jax.ShapeDtypeStruct((2, 512, 1024), BF),
            jax.ShapeDtypeStruct((1024, 1024), BF),
            jax.ShapeDtypeStruct((64, 1024), F32),
            jax.ShapeDtypeStruct((64, 1024), F32),
        ),
        in_specs=[hbm, hbm, hbm, hbm, vmem, vmem, smem, smem, smem, hbm],
        out_specs=(hbm,) * 5,
        scratch_shapes=[
            v((1024, 1024), BF),
            v((1024, 1024), BF),
            v((2, 512, 1024), BF),
            v((2, 512, 1024), BF),
            v((2, 8, 512, 128), BF),
            v((2, 8, 512, 128), BF),
            v((2, 8, 512, 512), BF),
            v((8, 4, 4, 64, 256), BF),
            v((8, 1024, 128), BF),
            v((8, 1024, 128), BF),
            v((5, 1024, 128), F32),
            v((2, 3, 1024, 128), BF),
            v((2, 3, 1024, 128), BF),
            v((2, 512, 128), BF),
            v((2, 512, 128), BF),
            v((2, 512, 128), BF),
            v((2, 128, 512), F32),
            v((2, 128, 512), F32),
            v((2, 128, 512), BF),
            v((2, 128, 512), BF),
            v((2, 4, 2, 1024, 128), BF),
            v((8, 2, 4, 4, 64, 128), BF),
            v((8, 2, 3, 4, 64, 128), BF),
            v((8, 2, 3, 64, 128), BF),
            v((2, 8, 512, 128), F32),
            v((2, 512, 1024), BF),
            v((2, 512, 1024), BF),
            v((1024, 1024), BF),
            v((2, 64, 1024), F32),
            pltpu.SemaphoreType.DMA((MESSAGES,)),
            pltpu.SemaphoreType.DMA((MESSAGES,)),
            pltpu.SemaphoreType.DMA((32,)),
        ],
        compiler_params=pltpu.CompilerParams(
            collective_id=0, has_side_effects=True, vmem_limit_bytes=62 * 1024 * 1024
        ),
    )(
        queries,
        features.reshape(1024, 1024),
        key_weight,
        value_weight,
        query_gain.reshape(1, 128),
        key_gain.reshape(1, 128),
        tile_count,
        image_seq,
        text_len,
        cotangent,
    )
    context, query_grad, feature_grad, key_w, value_w = finish(
        context, query_grad, feature_grad, key_w, value_w
    )
    return context, query_grad, feature_grad.reshape(2, 512, 1024), key_w, value_w


def solution(mesh):
    in_specs = (
        P("dp", None, "mp"),
        P("dp", None, "mp"),
        P(("mp", "dp"), None),
        P(("mp", "dp"), None),
        P(),
        P(),
        P("dp"),
        P("dp"),
        P("dp"),
        P("dp", None, "mp"),
    )
    out_specs = (
        P("dp", None, "mp"),
        P("dp", None, "mp"),
        P("dp", None, "mp"),
        P(("mp", "dp"), None),
        P(("mp", "dp"), None),
    )
    return jax.shard_map(
        per_device, mesh=mesh, in_specs=in_specs, out_specs=out_specs, check_vma=False
    )
```

```python
import functools
import math

import jax
import jax.numpy as jnp
from jax import lax
from jax.experimental import pallas as pl
from jax.experimental.pallas import tpu as pltpu
from jax.sharding import PartitionSpec as P

KV_HEADS = 8
TT = 128
EPSILON = 1e-05
MESH = pl.DeviceIdType.MESH
BF = jnp.bfloat16
F32 = jnp.float32
MESSAGES = 320
DIRECT = (0,)


def dot_nn(a, b):
    return jnp.dot(a, b, preferred_element_type=F32)


def dot_nt(a, b):
    return lax.dot_general(a, b, (((1,), (1,)), ((), ())), preferred_element_type=F32)


def dot_tn(a, b):
    return lax.dot_general(a, b, (((0,), (0,)), ((), ())), preferred_element_type=F32)


def kernel(
    queries,
    features,
    key_weight,
    value_weight,
    query_gain,
    key_gain,
    tile_count,
    image_seq,
    text_len,
    cotangent,
    context_out,
    query_out,
    feature_out,
    key_w_out,
    value_w_out,
    fv,
    ft,
    qv,
    cv,
    qh,
    cotp,
    ev,
    wb,
    part_tx,
    part_rx,
    total,
    z_tx,
    z_rx,
    kh,
    vh,
    tok,
    dvacc,
    dkacc,
    kt,
    vt,
    dkv,
    gr,
    rx1,
    rx2,
    inner,
    ctx_st,
    qg_st,
    fg_st,
    wg_st,
    send_sem,
    recv_sem,
    load_sem,
):
    dp, mp = lax.axis_index("dp"), lax.axis_index("mp")
    y, x = lax.div(dp, 4), lax.rem(dp, 4)
    z, core = lax.div(mp, 2), lax.rem(mp, 2)
    x1, x2, x3 = (lax.rem(x + k, 4) for k in (1, 2, 3))
    y1, y2, y3 = (lax.rem(y + k, 4) for k in (1, 2, 3))
    z1, z2, z3 = (lax.rem(z + k, 4) for k in (1, 2, 3))
    to_xp = {"dp": y * 4 + x1, "mp": mp}
    to_xm = {"dp": y * 4 + x3, "mp": mp}
    to_yp = {"dp": y1 * 4 + x, "mp": mp}
    to_ym = {"dp": y3 * 4 + x, "mp": mp}
    to_zp = {"dp": dp, "mp": z1 * 2 + core}
    to_zm = {"dp": dp, "mp": z3 * 2 + core}
    to_x2 = {"dp": y * 4 + x2, "mp": mp}
    to_y2 = {"dp": y2 * 4 + x, "mp": mp}
    to_z2 = {"dp": dp, "mp": z2 * 2 + core}
    to_pt = {"dp": dp, "mp": z * 2 + 1 - core}
    scale = 1.0 / math.sqrt(128)
    count = [0]
    sent = []

    class Msg:
        def __init__(self, src, dst, dev, local):
            k = count[0]
            count[0] += 1
            self.copy = pltpu.make_async_remote_copy(
                src_ref=src,
                dst_ref=dst,
                send_sem=send_sem.at[k],
                recv_sem=recv_sem.at[k],
                device_id=dev,
                device_id_type=MESH,
            )
            self.local, self.dev, self.k = local, dev, k
            self.copy.start()
            sent.append(self.copy)

        def arrive(self):
            pltpu.make_async_remote_copy(
                src_ref=self.local,
                dst_ref=self.local,
                send_sem=send_sem.at[self.k],
                recv_sem=recv_sem.at[self.k],
                device_id=self.dev,
                device_id_type=MESH,
            ).wait_recv()

    offs = (2, 1, 3, 0)
    own_loads = []
    for n in range(8):
        src = key_weight if n < 4 else value_weight
        zc = lax.rem(z + offs[n % 4], 4)
        for p in range(2):
            head = zc * 2 + (core if p == 0 else 1 - core)
            col = pl.multiple_of(head * 128, 128)
            c = pltpu.make_async_copy(
                src.at[:, pl.ds(col, 128)],
                wb.at[n, y, x, :, pl.ds(p * 128, 128)],
                load_sem.at[len(own_loads)],
            )
            c.start()
            own_loads.append(c)
    load_f = pltpu.make_async_copy(features, fv, load_sem.at[16])
    load_q = pltpu.make_async_copy(queries, qv, load_sem.at[17])
    load_c = pltpu.make_async_copy(cotangent, cv, load_sem.at[18])
    load_q.start()
    load_f.start()
    load_c.start()

    barrier = pltpu.get_barrier_semaphore()
    for dev in (to_xp, to_xm, to_x2, to_yp, to_ym, to_y2, to_zp, to_zm, to_z2, to_pt):
        pl.semaphore_signal(barrier, inc=1, device_id=dev, device_id_type=MESH)
    pl.semaphore_wait(barrier, 10)

    first, group, far = {}, {}, {}
    spans = ((0, 1), (1, 3), (4, 4))

    def pa(span, xx):
        n0, cnt = span
        return wb.at[n0 : n0 + cnt, y, xx, 0:32]

    def pb(span, yy):
        n0, cnt = span
        return wb.at[n0 : n0 + cnt, yy, x, 32:64]

    def s0(k):
        sp = spans[k]
        for c in own_loads[2 * sp[0] : 2 * (sp[0] + sp[1])]:
            c.wait()
        first[k] = (
            Msg(pa(sp, x), pa(sp, x), to_xp, pa(sp, x3)),
            Msg(pa(sp, x), pa(sp, x), to_xm, pa(sp, x1)),
            Msg(pb(sp, y), pb(sp, y), to_yp, pb(sp, y3)),
            Msg(pb(sp, y), pb(sp, y), to_ym, pb(sp, y1)),
            Msg(pa(sp, x), pa(sp, x), to_x2, pa(sp, x2)),
            Msg(pb(sp, y), pb(sp, y), to_y2, pb(sp, y2)),
        )

    def s1(k):
        for msg in first[k]:
            msg.arrive()

    def ga(n, yy, lo=0, hi=4):
        return wb.at[n, yy, lo:hi, 0:32]

    def gb(n, xx, lo=0, hi=4):
        return wb.at[n, lo:hi, xx, 32:64]

    def s2(n):
        group[n] = (
            Msg(ga(n, y), ga(n, y), to_yp, ga(n, y3)),
            Msg(ga(n, y), ga(n, y), to_ym, ga(n, y1)),
            Msg(gb(n, x), gb(n, x), to_xp, gb(n, x3)),
            Msg(gb(n, x), gb(n, x), to_xm, gb(n, x1)),
        )
        if n in DIRECT:
            far[n] = (
                Msg(ga(n, y), ga(n, y), to_y2, ga(n, y2)),
                Msg(gb(n, x), gb(n, x), to_x2, gb(n, x2)),
            )

    def s3(n):
        for msg in group[n]:
            msg.arrive()
        if n not in DIRECT:
            far[n] = (
                Msg(ga(n, y3, 0, 2), ga(n, y3, 0, 2), to_yp, ga(n, y2, 0, 2)),
                Msg(ga(n, y1, 2, 4), ga(n, y1, 2, 4), to_ym, ga(n, y2, 2, 4)),
                Msg(gb(n, x3, 0, 2), gb(n, x3, 0, 2), to_xp, gb(n, x2, 0, 2)),
                Msg(gb(n, x1, 2, 4), gb(n, x1, 2, 4), to_xm, gb(n, x2, 2, 4)),
            )

    def s4(n):
        for msg in far[n]:
            msg.arrive()

    part, sums = {}, {}

    def t_of(n):
        return n % 4 if n % 4 < 3 else 3 + n // 4

    def proj(n):
        def block(i, carry):
            rows = pl.ds(pl.multiple_of(i * 256, 256), 256)
            out = dot_nn(fv[rows, :], wb[n].reshape(1024, 256))
            total[t_of(n), rows, :] = out[:, :128]
            part_tx[n, rows, :] = out[:, 128:].astype(BF)
            return carry

        lax.fori_loop(0, 4, block, 0, unroll=True)
        part[n] = Msg(part_tx.at[n], part_rx.at[n], to_pt, part_rx.at[n])

    def z_step(n):
        k, j, t = n // 4, n % 4, t_of(n)
        part[n].arrive()
        value = total[t] + part_rx[n].astype(F32)
        total[t] = value
        if j == 0:
            z_tx[k, 0] = value.astype(BF)
            for h, dev in ((0, to_zp), (1, to_zm)):
                r = slice(h * 512, (h + 1) * 512)
                sums[k, 0, h] = Msg(z_tx.at[k, 0, r], z_rx.at[k, 0, r], dev, z_rx.at[k, 0, r])
        elif j < 3:
            h = 2 - j
            r = slice(h * 512, (h + 1) * 512)
            z_tx[k, j, r] = value[r].astype(BF)
            dev = (to_zp, to_zm)[j - 1]
            sums[k, j, h] = Msg(z_tx.at[k, j, r], z_rx.at[k, j, r], dev, z_rx.at[k, j, r])

    def z_relay(k):
        for h, dev in ((0, to_zp), (1, to_zm)):
            j = h + 1
            sums[k, 0, h].arrive()
            r = slice(h * 512, (h + 1) * 512)
            z_tx[k, j, r] = (total[j, r] + z_rx[k, 0, r].astype(F32)).astype(BF)
            sums[k, j, h] = Msg(z_tx.at[k, j, r], z_rx.at[k, j, r], dev, z_rx.at[k, j, r])

    def z_last(k):
        t = 3 + k
        for j in (1, 2):
            for h in range(2):
                sums[k, j, h].arrive()
        total[t] = total[t] + (z_rx[k, 1].astype(F32) + z_rx[k, 2].astype(F32))

    seqs = [image_seq[0], image_seq[1]]
    tiles = [tile_count[0], tile_count[1]]
    lens = [text_len[0], text_len[1]]
    own_len = [jnp.where(s == 0, lens[0], lens[1]) for s in seqs]
    same = jnp.where(seqs[0] == seqs[1], 1.0, 0.0).astype(F32)
    weight = [[jnp.where(seqs[i] == s, 1.0, 0.0).astype(F32) for s in range(2)] for i in range(2)]
    text_at = lax.broadcasted_iota(jnp.int32, (512, 128), 0)

    def norm_queries(s):
        gain = query_gain[...]

        def block(i, carry):
            rows = pl.ds(pl.multiple_of(i * 128, 128), 128)
            for g in range(8):
                q = qv[s, rows, g * 128 : (g + 1) * 128].astype(F32)
                inv = lax.rsqrt(jnp.mean(q * q, axis=-1, keepdims=True) + EPSILON)
                qh[s, g, rows, :] = (gain * q * inv).astype(BF)
            return carry

        lax.fori_loop(0, 4, block, 0, unroll=True)

    def turn_features():
        for i in range(4):
            ft[:, i * 256 : (i + 1) * 256] = fv[i * 256 : (i + 1) * 256, :].T

    def set_masks():
        for i in range(2):
            tok[i] = jnp.where(text_at < tiles[i] * TT, 1.0, 0.0).astype(BF)
            dvacc[i] = jnp.zeros((128, 512), F32)
            dkacc[i] = jnp.zeros((128, 512), F32)

    def key_final():
        raw = total[3]
        inv = lax.rsqrt(jnp.mean(raw * raw, axis=-1, keepdims=True) + EPSILON)
        kh[...] = (key_gain[...] * raw * inv).astype(BF).reshape(2, 512, 128)
        for i in range(2):
            kt[i] = kh[i].T

    def value_final():
        vh[...] = total[4].astype(BF).reshape(2, 512, 128)
        for i in range(2):
            vt[i] = vh[i].T

    def soft(g0, g1):
        def one(g, carry):
            den = []
            for i in range(2):
                q = qh[seqs[i], g]
                e = jnp.exp2(dot_nn(q, kt[i]) * (scale * 1.4426950408889634)).astype(BF)
                ev[i, g] = e
                den.append(dot_nn(e, tok[i]))
            lane = pl.ds(pl.multiple_of(g * 128, 128), 128)
            for i in range(2):
                inv = 1.0 / (den[i] + same * den[1 - i])
                inner[i, g] = inv
                c = cv[seqs[i], :, lane].astype(F32) * inv
                c = jnp.where(text_at < own_len[i], c, 0.0).astype(BF)
                cotp[i, g] = c
                dvacc[i] += dot_tn(c, ev[i, g])
            return carry

        lax.fori_loop(g0, g1, one, 0)

    def back_context(g0, g1):
        def one(g, carry):
            lane = pl.ds(pl.multiple_of(g * 128, 128), 128)
            ctx = [dot_nn(ev[i, g], vh[i] * tok[i]) * inner[i, g] for i in range(2)]
            for i in range(2):
                full = ctx[i] + same * ctx[1 - i]
                fg_st[i * 512 : (i + 1) * 512, lane] = full.astype(BF)
                got = jnp.sum(cotp[i, g].astype(F32) * full, axis=-1, keepdims=True)
                inner[i, g] = jnp.broadcast_to(got, (512, 128))
            return carry

        lax.fori_loop(g0, g1, one, 0)

    def context_final():
        def one(g, carry):
            lane = pl.ds(pl.multiple_of(g * 128, 128), 128)
            full = [fg_st[i * 512 : (i + 1) * 512, lane].astype(F32) for i in range(2)]
            for s in range(2):
                out = jnp.where(seqs[1] == s, full[1], 0.0)
                out = jnp.where(seqs[0] == s, full[0], out)
                ctx_st[s, :, lane] = jnp.where(text_at < lens[s], out, 0.0).astype(BF)
            return carry

        lax.fori_loop(0, 8, one, 0)

    def back(i, g0, g1):
        def one(g, carry):
            grad_p = dot_nn(cotp[i, g], vt[i])
            less = jnp.concatenate([inner[i, g]] * 4, axis=1)
            ds = (ev[i, g].astype(F32) * (grad_p - less)).astype(BF)
            ev[i, g] = ds
            dkacc[i] += dot_tn(qh[seqs[i], g], ds)
            return carry

        lax.fori_loop(g0, g1, one, 0, unroll=2)

    def query_back(g0, g1):
        gain = query_gain[...]

        def one(g, carry):
            lane = pl.ds(pl.multiple_of(g * 128, 128), 128)
            dq = [dot_nn(ev[i, g], kh[i] * tok[i]) for i in range(2)]
            for s in range(2):
                got = gain * (weight[0][s] * dq[0] + weight[1][s] * dq[1]) * scale
                q = qv[s, :, lane].astype(F32)
                inv = lax.rsqrt(jnp.mean(q * q, axis=-1, keepdims=True) + EPSILON)
                dots = jnp.sum(got * q, axis=-1, keepdims=True)
                out = got * inv - q * (dots * (inv * inv * inv) * (1.0 / 128))
                qg_st[s, :, lane] = out.astype(BF)
            return carry

        lax.fori_loop(g0, g1, one, 0)

    near, across, over = {}, {}, {}

    def spread(k, i):
        r = slice(i * 512, (i + 1) * 512)
        own = dkv.at[k, 0, 0, r]
        near[k, i] = (
            Msg(own, dkv.at[k, 1, 0, r], to_zp, dkv.at[k, 1, 0, r]),
            Msg(own, dkv.at[k, 2, 0, r], to_zm, dkv.at[k, 2, 0, r]),
        )

    def spread_own(k):
        own = dkv.at[k, 0, 0]
        across[k, 0] = Msg(own, dkv.at[k, 0, 1], to_pt, dkv.at[k, 0, 1])
        over[k] = []

    def relay(k, i):
        for j, dev in ((1, to_zp), (2, to_zm)):
            near[k, i][j - 1].arrive()
            r = slice(i * 512 + (j - 1) * 256, i * 512 + j * 256)
            over[k].append(Msg(dkv.at[k, j, 0, r], dkv.at[k, 3, 0, r], dev, dkv.at[k, 3, 0, r]))

    def pass_near(k):
        for j in (1, 2):
            across[k, j] = Msg(dkv.at[k, j, 0], dkv.at[k, j, 1], to_pt, dkv.at[k, j, 1])

    def pass_far(k):
        for msg in over[k]:
            msg.arrive()
        across[k, 3] = Msg(dkv.at[k, 3, 0], dkv.at[k, 3, 1], to_pt, dkv.at[k, 3, 1])

    m1, m2 = {}, {}

    def w_of(k, j):
        return (3, 2, 1, 0)[j] + (4 if k == 0 else 0)

    def grad(k, j):
        t = k * 4 + j
        across[k, j].arrive()

        def block(i, carry):
            rows = pl.ds(pl.multiple_of(i * 256, 256), 256)
            cat = jnp.concatenate([dkv[k, j, 0], dkv[k, j, 1]], axis=1)
            out = dot_nn(ft[rows, :], cat).astype(BF)
            gr[t, 0, i] = out[:, :128].reshape(4, 64, 128)
            gr[t, 1, i] = out[:, 128:].reshape(4, 64, 128)
            return carry

        lax.fori_loop(0, 4, block, 0, unroll=True)
        a, b = gr.at[t, 0], gr.at[t, 1]
        r = [[rx1.at[t, h, e] for e in range(3)] for h in range(2)]
        m1[t] = (
            Msg(a.at[y1], r[0][0], to_yp, r[0][0]),
            Msg(a.at[y3], r[0][1], to_ym, r[0][1]),
            Msg(b.at[:, x1], r[1][0], to_xp, r[1][0]),
            Msg(b.at[:, x3], r[1][1], to_xm, r[1][1]),
            Msg(a.at[y2], r[0][2], to_y2, r[0][2]),
            Msg(b.at[:, x2], r[1][2], to_x2, r[1][2]),
        )

    def add(ref, h, t):
        value = ref[...].astype(F32)
        for e in range(3):
            value = value + rx1[t, h, e].astype(F32)
        ref[...] = value.astype(BF)

    def p2(t):
        a, b = gr.at[t, 0], gr.at[t, 1]
        for msg in m1[t]:
            msg.arrive()
        add(a.at[y], 0, t)
        add(b.at[:, x], 1, t)
        r = [[rx2.at[t, h, e] for e in range(3)] for h in range(2)]
        m2[t] = (
            Msg(a.at[y, x1], r[0][0], to_xp, r[0][0]),
            Msg(a.at[y, x3], r[0][1], to_xm, r[0][1]),
            Msg(b.at[y1, x], r[1][0], to_yp, r[1][0]),
            Msg(b.at[y3, x], r[1][1], to_ym, r[1][1]),
            Msg(a.at[y, x2], r[0][2], to_x2, r[0][2]),
            Msg(b.at[y2, x], r[1][2], to_y2, r[1][2]),
        )

    def p3(t):
        k, j = t // 4, t % 4
        for msg in m2[t]:
            msg.arrive()
        zc = (z, z3, z1, z2)[j]
        for h in range(2):
            head = zc * 2 + (core if h == 0 else 1 - core)
            lane = pl.ds(pl.multiple_of(head * 128, 128), 128)
            value = gr[t, h, y, x].astype(F32)
            for e in range(3):
                value = value + rx2[t, h, e].astype(F32)
            wg_st[k, :, lane] = value

    def feature_back(i0, i1):
        def block(i, carry):
            rows = pl.ds(pl.multiple_of(i * 256, 256), 256)
            acc = None
            for k in range(2):
                for j in range(4):
                    cat = jnp.concatenate([dkv[k, j, 0, rows], dkv[k, j, 1, rows]], axis=1)
                    term = dot_nt(cat, wb[w_of(k, j)].reshape(1024, 256))
                    acc = term if acc is None else acc + term
            fg_st[rows, :] = acc.astype(BF)
            return carry

        lax.fori_loop(i0, i1, block, 0, unroll=True)

    def value_grad(i):
        dkv[0, 0, 0, i * 512 : (i + 1) * 512] = (dvacc[i].T * tok[i].astype(F32)).astype(BF)

    def key_grad(i):
        gain = key_gain[...]
        got = gain * (dkacc[i].T * tok[i].astype(F32)) * scale
        raw = total[3, i * 512 : (i + 1) * 512]
        inv = lax.rsqrt(jnp.mean(raw * raw, axis=-1, keepdims=True) + EPSILON)
        dots = jnp.sum(got * raw, axis=-1, keepdims=True)
        out = got * inv - raw * (dots * (inv * inv * inv) * (1.0 / 128))
        dkv[1, 0, 0, i * 512 : (i + 1) * 512] = out.astype(BF)

    stores = []

    def store(src, dst):
        c = pltpu.make_async_copy(src, dst, load_sem.at[19 + len(stores)])
        c.start()
        stores.append(c)

    s0(0)
    s0(1)
    set_masks()
    load_q.wait()
    norm_queries(0)
    s1(0)
    s2(0)
    s1(1)
    s2(1)
    s2(2)
    s2(3)
    s0(2)
    norm_queries(1)
    load_f.wait()
    turn_features()
    load_c.wait()
    s3(0)
    s4(0)
    proj(0)
    s3(1)
    z_step(0)
    s3(2)
    s4(1)
    proj(1)
    s3(3)
    s1(2)
    s2(4)
    s2(5)
    s4(2)
    proj(2)
    z_step(1)
    s4(3)
    proj(3)
    z_step(2)
    z_relay(0)
    s2(6)
    s2(7)
    z_step(3)
    s3(4)
    s3(5)
    z_last(0)
    key_final()
    s3(6)
    soft(0, 2)
    s3(7)
    s4(4)
    proj(4)
    s4(5)
    proj(5)
    z_step(4)
    soft(2, 4)
    s4(6)
    proj(6)
    z_step(5)
    s4(7)
    proj(7)
    z_step(6)
    z_relay(1)
    soft(4, 6)
    z_step(7)
    soft(6, 8)
    value_grad(0)
    spread(0, 0)
    value_grad(1)
    spread(0, 1)
    spread_own(0)
    z_last(1)
    value_final()
    grad(0, 0)
    back_context(0, 8)
    relay(0, 0)
    back(0, 0, 4)
    relay(0, 1)
    pass_near(0)
    back(0, 4, 8)
    key_grad(0)
    spread(1, 0)
    grad(0, 1)
    grad(0, 2)
    pass_far(0)
    p2(0)
    back(1, 0, 8)
    key_grad(1)
    spread(1, 1)
    spread_own(1)
    grad(1, 0)
    relay(1, 0)
    grad(0, 3)
    p2(1)
    query_back(0, 4)
    relay(1, 1)
    pass_near(1)
    p2(2)
    context_final()
    store(ctx_st, context_out)
    grad(1, 1)
    grad(1, 2)
    pass_far(1)
    p2(3)
    p2(4)
    grad(1, 3)
    p3(0)
    p3(1)
    p3(2)
    p2(5)
    query_back(4, 8)
    store(qg_st, query_out)
    p3(3)
    p3(4)
    store(wg_st.at[0], value_w_out)
    feature_back(0, 2)
    store(fg_st.at[0:512], feature_out.at[0:512])
    p2(6)
    p2(7)
    feature_back(2, 4)
    store(fg_st.at[512:1024], feature_out.at[512:1024])
    p3(5)
    p3(6)
    p3(7)
    store(wg_st.at[1], key_w_out)
    for c in sent:
        c.wait_send()
    for c in stores:
        c.wait()


def finish_kernel(*refs):
    stage, sem = refs[10:15], refs[15]
    loads = [pltpu.make_async_copy(refs[k], stage[k], sem.at[0, k]) for k in range(5)]
    stores = [pltpu.make_async_copy(stage[k], refs[5 + k], sem.at[1, k]) for k in range(5)]
    for c in loads:
        c.start()
    for k in range(5):
        loads[k].wait()
        stores[k].start()
    for c in stores:
        c.wait()


def finish(*arrays):
    hbm = pl.BlockSpec(memory_space=pl.ANY)
    return pl.pallas_call(
        finish_kernel,
        out_shape=tuple(jax.ShapeDtypeStruct(a.shape, a.dtype) for a in arrays),
        in_specs=[hbm] * 5,
        out_specs=(hbm,) * 5,
        scratch_shapes=[pltpu.VMEM(a.shape, a.dtype) for a in arrays]
        + [pltpu.SemaphoreType.DMA((2, 5))],
        compiler_params=pltpu.CompilerParams(vmem_limit_bytes=60 * 1024 * 1024),
    )(*arrays)


def per_device(
    queries,
    features,
    key_weight,
    value_weight,
    query_gain,
    key_gain,
    tile_count,
    image_seq,
    text_len,
    cotangent,
):
    hbm = pl.BlockSpec(memory_space=pl.ANY)
    vmem = pl.BlockSpec(memory_space=pltpu.VMEM)
    smem = pl.BlockSpec(memory_space=pltpu.SMEM)
    v = pltpu.VMEM
    context, query_grad, feature_grad, key_w, value_w = pl.pallas_call(
        kernel,
        out_shape=(
            jax.ShapeDtypeStruct((2, 512, 1024), BF),
            jax.ShapeDtypeStruct((2, 512, 1024), BF),
            jax.ShapeDtypeStruct((1024, 1024), BF),
            jax.ShapeDtypeStruct((64, 1024), F32),
            jax.ShapeDtypeStruct((64, 1024), F32),
        ),
        in_specs=[hbm, hbm, hbm, hbm, vmem, vmem, smem, smem, smem, hbm],
        out_specs=(hbm,) * 5,
        scratch_shapes=[
            v((1024, 1024), BF),
            v((1024, 1024), BF),
            v((2, 512, 1024), BF),
            v((2, 512, 1024), BF),
            v((2, 8, 512, 128), BF),
            v((2, 8, 512, 128), BF),
            v((2, 8, 512, 512), BF),
            v((8, 4, 4, 64, 256), BF),
            v((8, 1024, 128), BF),
            v((8, 1024, 128), BF),
            v((5, 1024, 128), F32),
            v((2, 3, 1024, 128), BF),
            v((2, 3, 1024, 128), BF),
            v((2, 512, 128), BF),
            v((2, 512, 128), BF),
            v((2, 512, 128), BF),
            v((2, 128, 512), F32),
            v((2, 128, 512), F32),
            v((2, 128, 512), BF),
            v((2, 128, 512), BF),
            v((2, 4, 2, 1024, 128), BF),
            v((8, 2, 4, 4, 64, 128), BF),
            v((8, 2, 3, 4, 64, 128), BF),
            v((8, 2, 3, 64, 128), BF),
            v((2, 8, 512, 128), F32),
            v((2, 512, 1024), BF),
            v((2, 512, 1024), BF),
            v((1024, 1024), BF),
            v((2, 64, 1024), F32),
            pltpu.SemaphoreType.DMA((MESSAGES,)),
            pltpu.SemaphoreType.DMA((MESSAGES,)),
            pltpu.SemaphoreType.DMA((32,)),
        ],
        compiler_params=pltpu.CompilerParams(
            collective_id=0, has_side_effects=True, vmem_limit_bytes=62 * 1024 * 1024
        ),
    )(
        queries,
        features.reshape(1024, 1024),
        key_weight,
        value_weight,
        query_gain.reshape(1, 128),
        key_gain.reshape(1, 128),
        tile_count,
        image_seq,
        text_len,
        cotangent,
    )
    context, query_grad, feature_grad, key_w, value_w = finish(
        context, query_grad, feature_grad, key_w, value_w
    )
    return context, query_grad, feature_grad.reshape(2, 512, 1024), key_w, value_w


def solution(mesh):
    in_specs = (
        P("dp", None, "mp"),
        P("dp", None, "mp"),
        P(("mp", "dp"), None),
        P(("mp", "dp"), None),
        P(),
        P(),
        P("dp"),
        P("dp"),
        P("dp"),
        P("dp", None, "mp"),
    )
    out_specs = (
        P("dp", None, "mp"),
        P("dp", None, "mp"),
        P("dp", None, "mp"),
        P(("mp", "dp"), None),
        P(("mp", "dp"), None),
    )
    return jax.shard_map(
        per_device, mesh=mesh, in_specs=in_specs, out_specs=out_specs, check_vma=False
    )
```
